32 devices in a mesh: groups: 2 (over y), rows: 4 (over z), section: 2 (over x), feat: 2 (over core).
Axes of the slice: x: 2, y: 2, z: 4, core: 2. Of those that a mesh axis runs over, the one named last changes fastest.
Arguments:
- test_rows: bfloat16 [3, 256, 8, 512], P(None, ('groups', 'rows'), 'feat'), parts along dimension 1, may hold values from -6 to 6
- train_cache: bfloat16 [2, 2, 32, 8, 512], P('section', None, ('groups', 'rows'), 'feat'), parts along dimension 2, may hold values from -6 to 6
- pattern: int32 [8, 8], replicated, may hold values 0 or 1
- feat_qkv: bfloat16 [2, 512, 1536], P('section'), may hold values from -0.25 to 0.25
- feat_out: bfloat16 [2, 512, 512], P('section'), may hold values from -0.25 to 0.25
- item_query: bfloat16 [2, 512, 512], P('section'), may hold values from -0.25 to 0.25
- item_out: bfloat16 [2, 512, 512], P('section'), may hold values from -0.25 to 0.25
- gains: float32 [2, 2, 512], P('section'), may hold values from 0.5 to 1.5
Outputs:
- hidden: bfloat16 [2, 3, 256, 8, 512], P('section', None, ('groups', 'rows'), 'feat'), parts along dimension 2
The draws below stay inside these ranges and needn't reach their ends.
There are 2 independent parts, one for each index of `groups`. The reference program is written for one: setup_inputs(seed, part) draws one part's arguments, and reference() takes and returns one part's arrays. A program takes and returns all parts, laid end to end along the dimension named above; an argument that names none is the same for every part. Nothing has to cross between parts.
All inputs are finite; a program needn't handle non-finite values.
Results may differ from the reference program's by a relative error of at most 0.02.
Values may be sent and summed in bfloat16 or wider, within the bound.
A program may use at most 64 MiB of HBM per device.

```python
import jax
import jax.numpy as jnp
from jax import lax

D = 512
HEADS = 8
MICRO = 3
LAYERS = 2
G = 8
TEST_ROWS = 128
TRAIN = 16


def with_ends(values, rng, least, high):
    longest = values.shape.index(max(values.shape))
    spots = []
    for shift in (0, 1):
        where = [jax.random.randint(jax.random.fold_in(rng, axis), (), 0, length) for axis, length in enumerate(values.shape)]
        where[longest] = (where[longest] + shift) % values.shape[longest]
        spots.append(tuple(where))
    return values.at[spots[0]].set(least).at[spots[1]].set(high)


def levels(key, shape, split, smallest, largest):
    level, own = 1.0, jax.random.fold_in(key, 6)
    for axis_at, parts in split:
        draws = jnp.exp(jax.random.uniform(jax.random.fold_in(own, axis_at), (parts,), jnp.float32, smallest / len(split), largest / len(split)))
        level = level * jnp.repeat(draws, shape[axis_at] // parts).reshape([-1 if axis == axis_at else 1 for axis in range(len(shape))])
    return level


def normal_values(own_key, shape, deviation, reach, cuts=(), kind=jnp.bfloat16):
    entries = deviation * jax.random.normal(own_key, shape, jnp.float32)
    if cuts:
        entries = entries * levels(own_key, shape, cuts, -0.22, 0.18)
    return jnp.clip(entries, -reach, reach).astype(kind)


def setup_inputs(seed: int = 0, part: int = 0) -> dict:
    splits = jax.random.split(jax.random.key(seed), 9)
    part_splits = jax.random.split(jax.random.fold_in(splits[8], part), 9)
    return {
        "test_rows": normal_values(part_splits[0], (MICRO, TEST_ROWS, G, D), 1.0, 6.0, ((1, 4), (2, 2))),
        "train_cache": normal_values(part_splits[1], (LAYERS, 2, TRAIN, G, D), 1.0, 6.0, ((0, 2), (2, 4), (3, 2))),
        "pattern": with_ends((jax.random.randint(splits[2], (G, G), 0, 2) < 1).astype(jnp.int32), jax.random.fold_in(splits[2], 1), 0, 1),
        "feat_qkv": normal_values(splits[3], (LAYERS, D, 3 * D), D ** -0.5, 0.25, ((0, 2),)),
        "feat_out": normal_values(splits[4], (LAYERS, D, D), D ** -0.5, 0.25, ((0, 2),)),
        "item_query": normal_values(splits[5], (LAYERS, D, D), D ** -0.5, 0.25, ((0, 2),)),
        "item_out": normal_values(splits[6], (LAYERS, D, D), D ** -0.5, 0.25, ((0, 2),)),
        "gains": jnp.clip(1.0 + 0.1 * jax.random.normal(splits[7], (LAYERS, 2, D), jnp.float32), 0.5, 1.5),
    }


HIGH = lax.Precision.HIGHEST

def normed(x, gain):
    mean_sq = lax.optimization_barrier(jnp.mean(x * x, axis=-1, keepdims=True))
    return x * lax.rsqrt(mean_sq + 1e-06) * gain

def one_layer(h, allowed, wqkv, wout, wquery, witem, gain_pair, cache):
    rows_n, groups, width = h.shape
    heads = HEADS
    head_dim = width // heads
    scale = 1.0 / head_dim ** 0.5
    a = normed(h, gain_pair[0]).astype(jnp.bfloat16).reshape(rows_n * groups, width)
    qkv = jnp.dot(a, wqkv, preferred_element_type=jnp.float32).astype(jnp.bfloat16)
    qkv = qkv.reshape(rows_n, groups, 3, heads, head_dim).astype(jnp.float32)
    query, keys, values = (qkv[:, :, 0], qkv[:, :, 1], qkv[:, :, 2])
    scores = jnp.einsum('rihd,rjhd->rhij', query, keys, precision=HIGH) * scale
    scores = jnp.where(allowed[None, None], scores, -1e+30)
    weights = jax.nn.softmax(scores, axis=-1).astype(jnp.bfloat16).astype(jnp.float32)
    mixed = jnp.einsum('rhij,rjhd->rihd', weights, values, precision=HIGH).astype(jnp.bfloat16)
    h1 = h + jnp.dot(mixed.reshape(rows_n * groups, width), wout, preferred_element_type=jnp.float32).reshape(rows_n, groups, width)
    b = normed(h1, gain_pair[1]).astype(jnp.bfloat16).reshape(rows_n * groups, width)
    item_q = jnp.dot(b, wquery, preferred_element_type=jnp.float32).astype(jnp.bfloat16)
    item_q = item_q.reshape(rows_n, groups, heads, head_dim).astype(jnp.float32)
    train_n = cache.shape[1]
    train_k = cache[0].astype(jnp.float32).reshape(train_n, groups, heads, head_dim)
    train_v = cache[1].astype(jnp.float32).reshape(train_n, groups, heads, head_dim)
    item_s = jnp.einsum('rghd,nghd->rghn', item_q, train_k, precision=HIGH) * scale
    probs = jax.nn.softmax(item_s, axis=-1)
    item_mix = jnp.einsum('rghn,nghd->rghd', probs, train_v, precision=HIGH).astype(jnp.bfloat16)
    item_term = jnp.dot(item_mix.reshape(rows_n * groups, width), witem, preferred_element_type=jnp.float32)
    return (h1 + item_term.reshape(rows_n, groups, width)).astype(jnp.bfloat16)

def reference(test_rows, train_cache, pattern, feat_qkv, feat_out, item_query, item_out, gains):
    groups = pattern.shape[0]
    allowed = (pattern != 0) | jnp.eye(groups, dtype=bool)
    per_layer = []
    states = [test_rows[m] for m in range(MICRO)]
    for layer in range(LAYERS):
        outs_now = []
        for m in range(MICRO):
            result = one_layer(states[m].astype(jnp.float32), allowed, feat_qkv[layer], feat_out[layer], item_query[layer], item_out[layer], gains[layer], train_cache[layer])
            outs_now.append(result)
        states = outs_now
        per_layer.append(jnp.stack(outs_now, axis=0))
    return jnp.stack(per_layer, axis=0)
```

```python
import functools
import math

import jax
import jax.numpy as jnp
from jax import lax
from jax.experimental import pallas as pl
from jax.experimental.pallas import tpu as pltpu
from jax.sharding import PartitionSpec as P

HEADS = 8
MESH = pl.DeviceIdType.MESH
F32 = jnp.float32
BF16 = jnp.bfloat16
EXCLUDED = -1e30


def iota(shape, dim):
    return lax.broadcasted_iota(jnp.int32, shape, dim)


def normed(x, gain):
    mean_sq = jnp.mean(x * x, axis=-1, keepdims=True)
    return (x * lax.rsqrt(mean_sq + 1e-06) * gain).astype(BF16)


def dot(a, b):
    return jnp.dot(a, b, preferred_element_type=F32)


def dot_t(a, b):
    return lax.dot_general(a, b, (((1,), (1,)), ((), ())), preferred_element_type=F32)


def kernel(
    sizes, rows_hbm, cache_hbm, pattern_ref, qkv_hbm, out_hbm, query_hbm, item_hbm, gains_ref, hidden_hbm,
    x_in, wqkv, wout, wquery, witem, h_buf, h_out, q_buf, kv_buf, cache_buf, k_stack, v_stack, feat_bias, item_bias, staged,
    weight_sem, x_sem, own_sem, out_sem, kv_send, kv_recv, cache_send, cache_recv, h_send, h_recv,
):
    sections, row_devs = sizes
    micro, test_n, gd, width = x_in.shape
    tokens = test_n * gd
    pair_w = 2 * (width // HEADS)
    pairs = width // pair_w
    half = tokens // 2
    half_rows = test_n // 2
    train_dev = cache_buf.shape[2]
    nk = row_devs * train_dev * gd
    factor = math.log2(math.e) / math.sqrt(width // HEADS)

    section = lax.axis_index("section")
    row = lax.axis_index("rows")
    feat = lax.axis_index("feat")
    partner = 1 - feat
    first = section == 0
    receives = section > 0
    sends = section < sections - 1

    weights = [
        pltpu.make_async_copy(src.at[0], dst, weight_sem.at[i])
        for i, (src, dst) in enumerate(
            [(qkv_hbm, wqkv), (out_hbm, wout), (query_hbm, wquery), (item_hbm, witem)]
        )
    ]

    def x_copy(m):
        return pltpu.make_async_copy(rows_hbm.at[m], x_in.at[m], x_sem.at[m])

    @pl.when(first)
    def _():
        for m in range(micro):
            x_copy(m).start()

    for copy in weights:
        copy.start()
    own_cache = pltpu.make_async_copy(cache_hbm.at[0], cache_buf.at[row], own_sem)
    own_cache.start()

    barrier = pltpu.get_barrier_semaphore()
    pl.semaphore_signal(barrier, inc=1, device_id={"feat": partner}, device_id_type=MESH)
    for off in range(1, row_devs):
        pl.semaphore_signal(
            barrier, inc=1, device_id={"rows": lax.rem(row + off, row_devs)}, device_id_type=MESH
        )

    @pl.when(receives)
    def _():
        pl.semaphore_signal(barrier, inc=1, device_id={"section": section - 1}, device_id_type=MESH)

    @pl.when(sends)
    def _():
        pl.semaphore_signal(barrier, inc=1, device_id={"section": section + 1}, device_id_type=MESH)

    pl.semaphore_wait(
        barrier, row_devs + jnp.where(receives, 1, 0) + jnp.where(sends, 1, 0)
    )

    def cache_copy(off):
        return pltpu.make_async_remote_copy(
            src_ref=cache_hbm.at[0], dst_ref=cache_buf.at[row],
            send_sem=cache_send.at[off - 1], recv_sem=cache_recv.at[row],
            device_id={"rows": lax.rem(row + off, row_devs)}, device_id_type=MESH,
        )

    def cache_arrival(off):
        source = lax.rem(row + off, row_devs)
        return pltpu.make_async_remote_copy(
            src_ref=cache_hbm.at[0], dst_ref=cache_buf.at[source],
            send_sem=cache_send.at[off - 1], recv_sem=cache_recv.at[source],
            device_id={"rows": source}, device_id_type=MESH,
        )

    for off in range(1, row_devs):
        cache_copy(off).start()

    def kv_copy(m):
        return pltpu.make_async_remote_copy(
            src_ref=kv_buf.at[m, 0], dst_ref=kv_buf.at[m, 1],
            send_sem=kv_send.at[m], recv_sem=kv_recv.at[m],
            device_id={"feat": partner}, device_id_type=MESH,
        )

    def h_copy(m, target):
        return pltpu.make_async_remote_copy(
            src_ref=h_out.at[m], dst_ref=h_buf.at[m],
            send_sem=h_send.at[m], recv_sem=h_recv.at[m],
            device_id={"section": target}, device_id_type=MESH,
        )

    def out_copy(m):
        return pltpu.make_async_copy(staged.at[m], hidden_hbm.at[0, m], out_sem.at[m])

    groups = 2 * gd
    q_at = iota((half, groups), 0) % gd + feat * gd
    pick_q = (q_at == iota((half, groups), 1)).astype(F32)
    key = iota((groups, 2 * half), 1)
    k_at = key % gd + jnp.where(key < half, feat, partner) * gd
    pick_k = (k_at == iota((groups, 2 * half), 0)).astype(F32)
    pattern = (pattern_ref[...] != 0).astype(F32)
    seen = dot(dot(pick_q, pattern), pick_k) > 0.5
    qi, ki = iota((half, 2 * half), 0), iota((half, 2 * half), 1)
    seen = seen | (qi == ki)
    seen = seen & (qi // gd == (ki % half) // gd)
    bias = jnp.where(seen, 0.0, EXCLUDED).astype(F32)
    feat_bias[...] = jnp.concatenate([bias, bias], axis=0)
    item_bias[...] = jnp.where(
        iota((tokens, 2 * nk), 0) % gd == iota((tokens, 2 * nk), 1) % gd, 0.0, EXCLUDED
    ).astype(F32)

    def project(m):
        @pl.when(first)
        def _():
            x_copy(m).wait()
            h_buf[m] = x_in[m].astype(F32).reshape(tokens, width).astype(BF16)

        @pl.when(receives)
        def _():
            h_copy(m, section - 1).wait_recv()

        a = normed(h_buf[m].astype(F32), gains_ref[0, 0:1, :])
        kv_buf[m, 0, :, :width] = dot(a, wqkv[:, width : 2 * width]).astype(BF16)
        kv_buf[m, 0, :, width:] = dot(a, wqkv[:, 2 * width :]).astype(BF16)
        kv_copy(m).start()
        q_buf[m] = dot(a, wqkv[:, :width]).astype(BF16)

    low_half = iota((half, pair_w), 1) < pair_w // 2
    ones = jnp.ones((2 * half, pair_w), BF16)

    def feature_mix(m):
        blocks = []
        for block in range(2):
            span = pl.ds(block * half, half)
            mixed = []
            for pair in range(pairs):
                lanes = slice(pair * pair_w, (pair + 1) * pair_w)
                v_lanes = slice(width + pair * pair_w, width + (pair + 1) * pair_w)
                q = q_buf[m, span, lanes]
                zero = jnp.zeros_like(q)
                q2 = jnp.concatenate([jnp.where(low_half, q, zero), jnp.where(low_half, zero, q)], axis=0)
                k = jnp.concatenate([kv_buf[m, 0, span, lanes], kv_buf[m, 1, span, lanes]], axis=0)
                v = jnp.concatenate([kv_buf[m, 0, span, v_lanes], kv_buf[m, 1, span, v_lanes]], axis=0)
                s = dot_t(q2, k) * factor + feat_bias[...]
                p = jnp.exp2(s - jnp.max(s, axis=-1, keepdims=True)).astype(BF16)
                o = dot(p, jnp.concatenate([v, ones], axis=1))
                o = o[:, :pair_w] / o[:, pair_w:]
                mixed.append(jnp.where(low_half, o[:half], o[half:]))
            blocks.append(jnp.concatenate(mixed, axis=1))
        return jnp.concatenate(blocks, axis=0).astype(BF16)

    low_keys = iota((tokens, 2 * nk), 1) < nk

    def item_mix(query):
        mixed = []
        for pair in range(pairs):
            lanes = slice(pair * pair_w, (pair + 1) * pair_w)
            s = dot_t(query[:, lanes], k_stack[pair]) * factor + item_bias[...]
            low = jnp.max(jnp.where(low_keys, s, -jnp.inf), axis=-1, keepdims=True)
            high = jnp.max(jnp.where(low_keys, -jnp.inf, s), axis=-1, keepdims=True)
            p = jnp.exp2(s - jnp.where(low_keys, low, high)).astype(BF16)
            o = dot(p, v_stack[pair])
            mixed.append(o[:, :pair_w] / o[:, pair_w:])
        return jnp.concatenate(mixed, axis=1).astype(BF16)

    weights[0].wait()
    project(0)

    def step(m, carry):
        @pl.when(m + 1 < micro)
        def _():
            project(m + 1)

        kv_copy(m).wait_recv()
        mixed = feature_mix(m)

        @pl.when(m == 0)
        def _():
            weights[1].wait()
            weights[2].wait()
            weights[3].wait()
            own_cache.wait()
            for off in range(1, row_devs):
                cache_arrival(off).wait_recv()
            side = iota((nk, pair_w), 1) < pair_w // 2
            one = jnp.where(side, 1.0, 0.0).astype(BF16)
            for pair in range(pairs):
                lanes = slice(pair * pair_w, (pair + 1) * pair_w)
                k = cache_buf[:, 0, :, :, lanes].astype(F32).reshape(nk, pair_w).astype(BF16)
                v = cache_buf[:, 1, :, :, lanes].astype(F32).reshape(nk, pair_w).astype(BF16)
                zero = jnp.zeros_like(k)
                k_stack[pair] = jnp.concatenate([jnp.where(side, k, zero), jnp.where(side, zero, k)], axis=0)
                v_stack[pair] = jnp.concatenate(
                    [
                        jnp.concatenate([jnp.where(side, v, zero), one], axis=1),
                        jnp.concatenate([jnp.where(side, zero, v), 1 - one], axis=1),
                    ],
                    axis=0,
                )

        h1 = h_buf[m].astype(F32) + dot(mixed, wout[...])
        b = normed(h1, gains_ref[0, 1:2, :])
        query = dot(b, wquery[...]).astype(BF16)
        result = h1 + dot(item_mix(query), witem[...])
        h_out[m] = result.astype(BF16)

        @pl.when(sends)
        def _():
            h_copy(m, section + 1).start()

        staged[m] = result.reshape(test_n, gd, width).astype(BF16)
        out_copy(m).start()
        return carry

    lax.fori_loop(0, micro, step, 0)

    for m in range(micro):
        kv_copy(m).wait_send()
        out_copy(m).wait()

    @pl.when(sends)
    def _():
        for m in range(micro):
            h_copy(m, section + 1).wait_send()

    for off in range(1, row_devs):
        cache_copy(off).wait_send()


def per_device(sizes, test_rows, train_cache, pattern, feat_qkv, feat_out, item_query, item_out, gains):
    sections, row_devs = sizes
    micro, test_n, gd, width = test_rows.shape
    train_dev = train_cache.shape[2]
    tokens = test_n * gd
    nk = row_devs * train_dev * gd
    pair_w = 2 * (width // HEADS)
    pairs = width // pair_w
    anywhere = pl.BlockSpec(memory_space=pl.ANY)
    vmem = pl.BlockSpec(memory_space=pltpu.VMEM)
    dma = pltpu.SemaphoreType.DMA
    return pl.pallas_call(
        functools.partial(kernel, sizes),
        out_shape=jax.ShapeDtypeStruct((1, micro, test_n, gd, width), BF16),
        in_specs=[anywhere, anywhere, vmem, anywhere, anywhere, anywhere, anywhere, vmem],
        out_specs=anywhere,
        scratch_shapes=[
            pltpu.VMEM((micro, test_n, gd, width), BF16),
            pltpu.VMEM((width, 3 * width), BF16),
            pltpu.VMEM((width, width), BF16),
            pltpu.VMEM((width, width), BF16),
            pltpu.VMEM((width, width), BF16),
            pltpu.VMEM((micro, tokens, width), BF16),
            pltpu.VMEM((micro, tokens, width), BF16),
            pltpu.VMEM((micro, tokens, width), BF16),
            pltpu.VMEM((micro, 2, tokens, 2 * width), BF16),
            pltpu.VMEM((row_devs, 2, train_dev, gd, width), BF16),
            pltpu.VMEM((pairs, 2 * nk, pair_w), BF16),
            pltpu.VMEM((pairs, 2 * nk, 2 * pair_w), BF16),
            pltpu.VMEM((tokens, tokens), F32),
            pltpu.VMEM((tokens, 2 * nk), F32),
            pltpu.VMEM((micro, test_n, gd, width), BF16),
            dma((4,)),
            dma((micro,)),
            dma(()),
            dma((micro,)),
            dma((micro,)),
            dma((micro,)),
            dma((row_devs - 1,)),
            dma((row_devs,)),
            dma((micro,)),
            dma((micro,)),
        ],
        compiler_params=pltpu.CompilerParams(
            collective_id=0, has_side_effects=True, vmem_limit_bytes=60 * 1024 * 1024
        ),
    )(test_rows, train_cache, pattern, feat_qkv, feat_out, item_query, item_out, gains)


def solution(mesh):
    sizes = (mesh.shape["section"], mesh.shape["rows"])
    return jax.shard_map(
        functools.partial(per_device, sizes),
        mesh=mesh,
        in_specs=(
            P(None, ("groups", "rows"), "feat", None),
            P("section", None, ("groups", "rows"), "feat", None),
            P(),
            P("section", None, None),
            P("section", None, None),
            P("section", None, None),
            P("section", None, None),
            P("section", None, None),
        ),
        out_specs=P("section", None, ("groups", "rows"), "feat", None),
        check_vma=False,
    )
```

```python
import functools
import math

import jax
import jax.numpy as jnp
from jax import lax
from jax.experimental import pallas as pl
from jax.experimental.pallas import tpu as pltpu
from jax.sharding import PartitionSpec as P

HEADS = 8
MESH = pl.DeviceIdType.MESH
F32 = jnp.float32
BF16 = jnp.bfloat16
EXCLUDED = -1e30


def iota(shape, dim):
    return lax.broadcasted_iota(jnp.int32, shape, dim)


def normed(x, gain):
    mean_sq = jnp.mean(x * x, axis=-1, keepdims=True)
    return (x * lax.rsqrt(mean_sq + 1e-06) * gain).astype(BF16)


def dot(a, b):
    return jnp.dot(a, b, preferred_element_type=F32)


def dot_t(a, b):
    return lax.dot_general(a, b, (((1,), (1,)), ((), ())), preferred_element_type=F32)


def kernel(
    sizes, rows_hbm, cache_hbm, pattern_ref, qkv_hbm, out_hbm, query_hbm, item_hbm, gains_ref, hidden_ref,
    x_in, wqkv, wout, wquery, witem, h_buf, h_out, q_buf, kv_buf, cache_buf, k_stack, v_stack, feat_bias, item_bias,
    weight_sem, x_sem, own_sem, kv_send, kv_recv, cache_send, cache_recv, h_send, h_recv,
):
    sections, row_devs = sizes
    micro, test_n, gd, width = x_in.shape
    tokens = test_n * gd
    pair_w = 2 * (width // HEADS)
    pairs = width // pair_w
    half = tokens // 2
    half_rows = test_n // 2
    train_dev = cache_buf.shape[2]
    nk = row_devs * train_dev * gd
    factor = math.log2(math.e) / math.sqrt(width // HEADS)

    section = lax.axis_index("section")
    row = lax.axis_index("rows")
    feat = lax.axis_index("feat")
    partner = 1 - feat
    first = section == 0
    receives = section > 0
    sends = section < sections - 1

    weights = [
        pltpu.make_async_copy(src.at[0], dst, weight_sem.at[i])
        for i, (src, dst) in enumerate(
            [(qkv_hbm, wqkv), (out_hbm, wout), (query_hbm, wquery), (item_hbm, witem)]
        )
    ]

    def x_copy(m):
        return pltpu.make_async_copy(rows_hbm.at[m], x_in.at[m], x_sem.at[m])

    @pl.when(first)
    def _():
        for m in range(micro):
            x_copy(m).start()

    for copy in weights:
        copy.start()
    own_cache = pltpu.make_async_copy(cache_hbm.at[0], cache_buf.at[row], own_sem)
    own_cache.start()

    barrier = pltpu.get_barrier_semaphore()
    pl.semaphore_signal(barrier, inc=1, device_id={"feat": partner}, device_id_type=MESH)
    for off in range(1, row_devs):
        pl.semaphore_signal(
            barrier, inc=1, device_id={"rows": lax.rem(row + off, row_devs)}, device_id_type=MESH
        )

    @pl.when(receives)
    def _():
        pl.semaphore_signal(barrier, inc=1, device_id={"section": section - 1}, device_id_type=MESH)

    @pl.when(sends)
    def _():
        pl.semaphore_signal(barrier, inc=1, device_id={"section": section + 1}, device_id_type=MESH)

    pl.semaphore_wait(
        barrier, row_devs + jnp.where(receives, 1, 0) + jnp.where(sends, 1, 0)
    )

    def cache_copy(off):
        return pltpu.make_async_remote_copy(
            src_ref=cache_hbm.at[0], dst_ref=cache_buf.at[row],
            send_sem=cache_send.at[off - 1], recv_sem=cache_recv.at[row],
            device_id={"rows": lax.rem(row + off, row_devs)}, device_id_type=MESH,
        )

    def cache_arrival(off):
        source = lax.rem(row + off, row_devs)
        return pltpu.make_async_remote_copy(
            src_ref=cache_hbm.at[0], dst_ref=cache_buf.at[source],
            send_sem=cache_send.at[off - 1], recv_sem=cache_recv.at[source],
            device_id={"rows": source}, device_id_type=MESH,
        )

    for off in range(1, row_devs):
        cache_copy(off).start()

    def kv_copy(m):
        return pltpu.make_async_remote_copy(
            src_ref=kv_buf.at[m, 0], dst_ref=kv_buf.at[m, 1],
            send_sem=kv_send.at[m], recv_sem=kv_recv.at[m],
            device_id={"feat": partner}, device_id_type=MESH,
        )

    def h_copy(m, target):
        return pltpu.make_async_remote_copy(
            src_ref=h_out.at[m], dst_ref=h_buf.at[m],
            send_sem=h_send.at[m], recv_sem=h_recv.at[m],
            device_id={"section": target}, device_id_type=MESH,
        )

    groups = 2 * gd
    q_at = iota((half, groups), 0) % gd + feat * gd
    pick_q = (q_at == iota((half, groups), 1)).astype(F32)
    key = iota((groups, 2 * half), 1)
    k_at = key % gd + jnp.where(key < half, feat, partner) * gd
    pick_k = (k_at == iota((groups, 2 * half), 0)).astype(F32)
    pattern = (pattern_ref[...] != 0).astype(F32)
    seen = dot(dot(pick_q, pattern), pick_k) > 0.5
    qi, ki = iota((half, 2 * half), 0), iota((half, 2 * half), 1)
    seen = seen | (qi == ki)
    seen = seen & (qi // gd == (ki % half) // gd)
    bias = jnp.where(seen, 0.0, EXCLUDED).astype(F32)
    feat_bias[...] = jnp.concatenate([bias, bias], axis=0)
    item_bias[...] = jnp.where(
        iota((tokens, 2 * nk), 0) % gd == iota((tokens, 2 * nk), 1) % gd, 0.0, EXCLUDED
    ).astype(F32)

    low_lanes = iota((tokens, width), 1) % pair_w < pair_w // 2

    def project(m):
        @pl.when(first)
        def _():
            x_copy(m).wait()
            h_buf[m] = x_in[m].astype(F32).reshape(tokens, width).astype(BF16)

        @pl.when(receives)
        def _():
            h_copy(m, section - 1).wait_recv()

        a = normed(h_buf[m].astype(F32), gains_ref[0, 0:1, :])
        kv_buf[m, 0, :, :width] = dot(a, wqkv[:, width : 2 * width]).astype(BF16)
        kv_buf[m, 0, :, width:] = dot(a, wqkv[:, 2 * width :]).astype(BF16)
        kv_copy(m).start()
        q = dot(a, wqkv[:, :width]) * factor
        low = jnp.where(low_lanes, q, 0.0).astype(BF16)
        high = jnp.where(low_lanes, 0.0, q).astype(BF16)
        for block in range(2):
            span = slice(block * half, (block + 1) * half)
            q_buf[m, block, :half] = low[span]
            q_buf[m, block, half:] = high[span]

    low_half = iota((half, pair_w), 1) < pair_w // 2
    ones = jnp.ones((2 * half, pair_w), BF16)

    def feature_mix(m):
        blocks = []
        for block in range(2):
            span = pl.ds(block * half, half)
            mixed = []
            for pair in range(pairs):
                lanes = slice(pair * pair_w, (pair + 1) * pair_w)
                v_lanes = slice(width + pair * pair_w, width + (pair + 1) * pair_w)
                q2 = q_buf[m, block, :, lanes]
                k = jnp.concatenate([kv_buf[m, 0, span, lanes], kv_buf[m, 1, span, lanes]], axis=0)
                v = jnp.concatenate([kv_buf[m, 0, span, v_lanes], kv_buf[m, 1, span, v_lanes]], axis=0)
                s = dot_t(q2, k) + feat_bias[...]
                p = jnp.exp2(s - jnp.max(s, axis=-1, keepdims=True)).astype(BF16)
                o = dot(p, jnp.concatenate([v, ones], axis=1))
                total = jnp.where(low_half, o[:half, pair_w:], o[half:, pair_w:])
                o = jnp.where(low_half, o[:half, :pair_w], o[half:, :pair_w])
                mixed.append(o * pl.reciprocal(total, approx=True))
            blocks.append(jnp.concatenate(mixed, axis=1))
        return jnp.concatenate(blocks, axis=0).astype(BF16)

    low_keys = iota((tokens, 2 * nk), 1) < nk

    def item_mix(query):
        mixed = []
        for pair in range(pairs):
            lanes = slice(pair * pair_w, (pair + 1) * pair_w)
            s = dot_t(query[:, lanes], k_stack[pair]) + item_bias[...]
            low = jnp.max(jnp.where(low_keys, s, -jnp.inf), axis=-1, keepdims=True)
            high = jnp.max(jnp.where(low_keys, -jnp.inf, s), axis=-1, keepdims=True)
            p = jnp.exp2(s - jnp.where(low_keys, low, high)).astype(BF16)
            o = dot(p, v_stack[pair])
            mixed.append(o[:, :pair_w] * pl.reciprocal(o[:, pair_w:], approx=True))
        return jnp.concatenate(mixed, axis=1).astype(BF16)

    weights[0].wait()
    project(0)

    def step(m, carry):
        @pl.when(m + 1 < micro)
        def _():
            project(m + 1)

        kv_copy(m).wait_recv()
        mixed = feature_mix(m)

        @pl.when(m == 0)
        def _():
            weights[1].wait()
            weights[2].wait()
            weights[3].wait()
            own_cache.wait()
            for off in range(1, row_devs):
                cache_arrival(off).wait_recv()
            side = iota((nk, pair_w), 1) < pair_w // 2
            one = jnp.where(side, 1.0, 0.0).astype(BF16)
            for pair in range(pairs):
                lanes = slice(pair * pair_w, (pair + 1) * pair_w)
                k = cache_buf[:, 0, :, :, lanes].astype(F32).reshape(nk, pair_w).astype(BF16)
                v = cache_buf[:, 1, :, :, lanes].astype(F32).reshape(nk, pair_w).astype(BF16)
                zero = jnp.zeros_like(k)
                k_stack[pair] = jnp.concatenate([jnp.where(side, k, zero), jnp.where(side, zero, k)], axis=0)
                v_stack[pair] = jnp.concatenate(
                    [
                        jnp.concatenate([jnp.where(side, v, zero), one], axis=1),
                        jnp.concatenate([jnp.where(side, zero, v), 1 - one], axis=1),
                    ],
                    axis=0,
                )

        h1 = h_buf[m].astype(F32) + dot(mixed, wout[...])
        b = normed(h1, gains_ref[0, 1:2, :])
        query = (dot(b, wquery[...]) * factor).astype(BF16)
        result = h1 + dot(item_mix(query), witem[...])
        h_out[m] = result.astype(BF16)

        @pl.when(sends)
        def _():
            h_copy(m, section + 1).start()

        hidden_ref[0, m] = result.reshape(test_n, gd, width).astype(BF16)
        return carry

    lax.fori_loop(0, micro, step, 0)

    for m in range(micro):
        kv_copy(m).wait_send()

    @pl.when(sends)
    def _():
        for m in range(micro):
            h_copy(m, section + 1).wait_send()

    for off in range(1, row_devs):
        cache_copy(off).wait_send()


def per_device(sizes, test_rows, train_cache, pattern, feat_qkv, feat_out, item_query, item_out, gains):
    sections, row_devs = sizes
    micro, test_n, gd, width = test_rows.shape
    train_dev = train_cache.shape[2]
    tokens = test_n * gd
    nk = row_devs * train_dev * gd
    pair_w = 2 * (width // HEADS)
    pairs = width // pair_w
    anywhere = pl.BlockSpec(memory_space=pltpu.HBM)
    vmem = pl.BlockSpec(memory_space=pltpu.VMEM)
    dma = pltpu.SemaphoreType.DMA
    return pl.pallas_call(
        functools.partial(kernel, sizes),
        out_shape=jax.ShapeDtypeStruct((1, micro, test_n, gd, width), BF16),
        in_specs=[anywhere, anywhere, vmem, anywhere, anywhere, anywhere, anywhere, vmem],
        out_specs=vmem,
        scratch_shapes=[
            pltpu.VMEM((micro, test_n, gd, width), BF16),
            pltpu.VMEM((width, 3 * width), BF16),
            pltpu.VMEM((width, width), BF16),
            pltpu.VMEM((width, width), BF16),
            pltpu.VMEM((width, width), BF16),
            pltpu.VMEM((micro, tokens, width), BF16),
            pltpu.VMEM((micro, tokens, width), BF16),
            pltpu.VMEM((micro, 2, tokens, width), BF16),
            pltpu.VMEM((micro, 2, tokens, 2 * width), BF16),
            pltpu.VMEM((row_devs, 2, train_dev, gd, width), BF16),
            pltpu.VMEM((pairs, 2 * nk, pair_w), BF16),
            pltpu.VMEM((pairs, 2 * nk, 2 * pair_w), BF16),
            pltpu.VMEM((tokens, tokens), F32),
            pltpu.VMEM((tokens, 2 * nk), F32),
            dma((4,)),
            dma((micro,)),
            dma(()),
            dma((micro,)),
            dma((micro,)),
            dma((row_devs - 1,)),
            dma((row_devs,)),
            dma((micro,)),
            dma((micro,)),
        ],
        compiler_params=pltpu.CompilerParams(
            collective_id=0, has_side_effects=True, vmem_limit_bytes=40 * 1024 * 1024
        ),
    )(test_rows, train_cache, pattern, feat_qkv, feat_out, item_query, item_out, gains)


def solution(mesh):
    sizes = (mesh.shape["section"], mesh.shape["rows"])
    return jax.shard_map(
        functools.partial(per_device, sizes),
        mesh=mesh,
        in_specs=(
            P(None, ("groups", "rows"), "feat", None),
            P("section", None, ("groups", "rows"), "feat", None),
            P(),
            P("section", None, None),
            P("section", None, None),
            P("section", None, None),
            P("section", None, None),
            P("section", None, None),
        ),
        out_specs=P("section", None, ("groups", "rows"), "feat", None),
        check_vma=False,
    )
```

```python
import functools
import math

import jax
import jax.numpy as jnp
from jax import lax
from jax.experimental import pallas as pl
from jax.experimental.pallas import tpu as pltpu
from jax.sharding import PartitionSpec as P

HEADS = 8
MESH = pl.DeviceIdType.MESH
F32 = jnp.float32
BF16 = jnp.bfloat16
EXCLUDED = -1e30


def iota(shape, dim):
    return lax.broadcasted_iota(jnp.int32, shape, dim)


def normed(x, gain):
    mean_sq = jnp.mean(x * x, axis=-1, keepdims=True)
    return (x * lax.rsqrt(mean_sq + 1e-06) * gain).astype(BF16)


def dot(a, b):
    return jnp.dot(a, b, preferred_element_type=F32)


def dot_t(a, b):
    return lax.dot_general(a, b, (((1,), (1,)), ((), ())), preferred_element_type=F32)


def kernel(
    sizes, rows_hbm, cache_hbm, pattern_ref, qkv_hbm, out_hbm, query_hbm, item_hbm, gains_ref, hidden_hbm,
    x_buf, wqkv, wout, wquery, witem, h_buf, h_out, cache_buf, k_stack, v_stack, feat_bias, item_bias, staged,
    weight_sem, x_sem, own_sem, out_sem, x_send, x_recv, cache_send, cache_recv, pass_send, pass_recv,
    h_send, h_recv, out_send, out_recv,
):
    sections, row_devs = sizes
    micro, feats, rows_n, gd, width = x_buf.shape
    half = rows_n * gd
    tokens = feats * half
    pair_w = 2 * (width // HEADS)
    pairs = width // pair_w
    train_dev = cache_buf.shape[3]
    nk = row_devs * train_dev * gd
    factor = math.log2(math.e) / math.sqrt(width // HEADS)

    section = lax.axis_index("section")
    row = lax.axis_index("rows")
    feat = lax.axis_index("feat")
    partner = 1 - feat
    first = section == 0
    receives = section > 0
    sends = section < sections - 1
    mine = pl.ds(feat * rows_n, rows_n)
    theirs = pl.ds(partner * rows_n, rows_n)

    weights = [
        pltpu.make_async_copy(src.at[0], dst, weight_sem.at[i])
        for i, (src, dst) in enumerate(
            [(qkv_hbm, wqkv), (out_hbm, wout), (query_hbm, wquery), (item_hbm, witem)]
        )
    ]

    def x_own(m):
        return pltpu.make_async_copy(rows_hbm.at[m, mine], x_buf.at[m, feat], x_sem.at[m])

    @pl.when(first)
    def _():
        for m in range(micro):
            x_own(m).start()

    for copy in weights:
        copy.start()
    own_cache = pltpu.make_async_copy(cache_hbm.at[0], cache_buf.at[feat, row], own_sem)
    own_cache.start()

    barrier = pltpu.get_barrier_semaphore()
    pl.semaphore_signal(barrier, inc=1, device_id={"feat": partner}, device_id_type=MESH)
    for off in range(1, row_devs):
        pl.semaphore_signal(
            barrier, inc=1, device_id={"rows": lax.rem(row + off, row_devs)}, device_id_type=MESH
        )

    @pl.when(receives)
    def _():
        pl.semaphore_signal(barrier, inc=1, device_id={"section": section - 1}, device_id_type=MESH)

    @pl.when(sends)
    def _():
        pl.semaphore_signal(barrier, inc=1, device_id={"section": section + 1}, device_id_type=MESH)

    pl.semaphore_wait(
        barrier, row_devs + jnp.where(receives, 1, 0) + jnp.where(sends, 1, 0)
    )

    def x_copy(m, source):
        return pltpu.make_async_remote_copy(
            src_ref=rows_hbm.at[m, theirs], dst_ref=x_buf.at[m, source],
            send_sem=x_send.at[m], recv_sem=x_recv.at[m],
            device_id={"feat": partner}, device_id_type=MESH,
        )

    def cache_copy(off):
        return pltpu.make_async_remote_copy(
            src_ref=cache_hbm.at[0], dst_ref=cache_buf.at[feat, row],
            send_sem=cache_send.at[off - 1], recv_sem=cache_recv.at[row],
            device_id={"rows": lax.rem(row + off, row_devs)}, device_id_type=MESH,
        )

    def cache_arrival(off):
        source = lax.rem(row + off, row_devs)
        return pltpu.make_async_remote_copy(
            src_ref=cache_hbm.at[0], dst_ref=cache_buf.at[feat, source],
            send_sem=cache_send.at[off - 1], recv_sem=cache_recv.at[source],
            device_id={"rows": source}, device_id_type=MESH,
        )

    def cache_pass(off, source_feat):
        source = lax.rem(row + off, row_devs)
        return pltpu.make_async_remote_copy(
            src_ref=cache_hbm.at[0] if off == 0 else cache_buf.at[feat, source],
            dst_ref=cache_buf.at[source_feat, source],
            send_sem=pass_send.at[off], recv_sem=pass_recv.at[off],
            device_id={"feat": partner}, device_id_type=MESH,
        )

    @pl.when(first)
    def _():
        x_copy(0, feat).start()

    for off in range(1, row_devs):
        cache_copy(off).start()

    @pl.when(first)
    def _():
        for m in range(1, micro):
            x_copy(m, feat).start()

    cache_pass(0, feat).start()

    def h_copy(m, target):
        return pltpu.make_async_remote_copy(
            src_ref=h_out.at[m], dst_ref=h_buf.at[m],
            send_sem=h_send.at[m], recv_sem=h_recv.at[m],
            device_id={"section": target}, device_id_type=MESH,
        )

    def out_own(m):
        return pltpu.make_async_copy(staged.at[m, feat], hidden_hbm.at[0, m, mine], out_sem.at[m])

    def out_copy(m, place):
        return pltpu.make_async_remote_copy(
            src_ref=staged.at[m, partner], dst_ref=hidden_hbm.at[0, m, place],
            send_sem=out_send.at[m], recv_sem=out_recv.at[m],
            device_id={"feat": partner}, device_id_type=MESH,
        )

    groups = feats * gd
    token = iota((tokens, groups), 0)
    pick_q = ((token // half) * gd + token % gd == iota((tokens, groups), 1)).astype(F32)
    token = iota((groups, tokens), 1)
    pick_k = ((token // half) * gd + token % gd == iota((groups, tokens), 0)).astype(F32)
    pattern = (pattern_ref[...] != 0).astype(F32)
    seen = dot(dot(pick_q, pattern), pick_k) > 0.5
    qi, ki = iota((tokens, tokens), 0), iota((tokens, tokens), 1)
    seen = (seen | (qi == ki)) & ((qi % half) // gd == (ki % half) // gd)
    bias = jnp.where(seen, 0.0, EXCLUDED).astype(F32)
    feat_bias[:tokens] = bias
    feat_bias[tokens:] = bias
    item_bias[...] = jnp.where(
        iota((half, 2 * nk), 0) % gd == iota((half, 2 * nk), 1) % gd, 0.0, EXCLUDED
    ).astype(F32)

    def pass_cache():
        for off in range(1, row_devs):
            cache_arrival(off).wait_recv()
            cache_pass(off, feat).start()

    def stack_cache():
        own_cache.wait()
        for off in range(row_devs):
            cache_pass(off, partner).wait_recv()
        side = iota((nk, pair_w), 1) < pair_w // 2
        one = jnp.where(side, 1.0, 0.0).astype(BF16)
        other = jnp.where(side, 0.0, 1.0).astype(BF16)
        for f in range(feats):
            for pair in range(pairs):
                lanes = slice(pair * pair_w, (pair + 1) * pair_w)
                k = cache_buf[f, :, 0, :, :, lanes].astype(F32).reshape(nk, pair_w)
                v = cache_buf[f, :, 1, :, :, lanes].astype(F32).reshape(nk, pair_w)
                k_stack[f, pair, :nk] = jnp.where(side, k, 0.0).astype(BF16)
                k_stack[f, pair, nk:] = jnp.where(side, 0.0, k).astype(BF16)
                v_stack[f, pair, :nk, :pair_w] = jnp.where(side, v, 0.0).astype(BF16)
                v_stack[f, pair, nk:, :pair_w] = jnp.where(side, 0.0, v).astype(BF16)
                v_stack[f, pair, :nk, pair_w:] = one
                v_stack[f, pair, nk:, pair_w:] = other

    low_half = iota((tokens, pair_w), 1) < pair_w // 2
    ones = jnp.ones((tokens, pair_w), BF16)

    def feature_mix(q, k, v):
        mixed = []
        for pair in range(pairs):
            lanes = slice(pair * pair_w, (pair + 1) * pair_w)
            q1 = q[:, lanes]
            q2 = jnp.concatenate(
                [jnp.where(low_half, q1, 0.0).astype(BF16), jnp.where(low_half, 0.0, q1).astype(BF16)], axis=0
            )
            s = dot_t(q2, k[:, lanes]) + feat_bias[...]
            p = jnp.exp2(s - jnp.max(s, axis=-1, keepdims=True)).astype(BF16)
            o = dot(p, jnp.concatenate([v[:, lanes], ones], axis=1))
            total = jnp.where(low_half, o[:tokens, pair_w:], o[tokens:, pair_w:])
            o = jnp.where(low_half, o[:tokens, :pair_w], o[tokens:, :pair_w])
            mixed.append((o * pl.reciprocal(total, approx=True)).astype(BF16))
        return jnp.concatenate(mixed, axis=1)

    low_keys = iota((half, 2 * nk), 1) < nk

    def item_mix(query):
        blocks = []
        for f in range(feats):
            mixed = []
            for pair in range(pairs):
                lanes = slice(pair * pair_w, (pair + 1) * pair_w)
                s = dot_t(query[f * half : (f + 1) * half, lanes], k_stack[f, pair]) + item_bias[...]
                low = jnp.max(jnp.where(low_keys, s, -jnp.inf), axis=-1, keepdims=True)
                high = jnp.max(jnp.where(low_keys, -jnp.inf, s), axis=-1, keepdims=True)
                p = jnp.exp2(s - jnp.where(low_keys, low, high)).astype(BF16)
                o = dot(p, v_stack[f, pair])
                mixed.append((o[:, :pair_w] * pl.reciprocal(o[:, pair_w:], approx=True)).astype(BF16))
            blocks.append(jnp.concatenate(mixed, axis=1))
        return jnp.concatenate(blocks, axis=0)

    @pl.when(receives)
    def _():
        pass_cache()
        stack_cache()

    weights[0].wait()
    weights[1].wait()
    weights[2].wait()
    weights[3].wait()

    def step(m, carry):
        @pl.when(first)
        def _():
            x_own(m).wait()
            x_copy(m, partner).wait_recv()
            h_buf[m] = x_buf[m].astype(F32).reshape(tokens, width).astype(BF16)

        @pl.when(receives)
        def _():
            h_copy(m, section - 1).wait_recv()

        h = h_buf[m].astype(F32)
        a = normed(h, gains_ref[0, 0:1, :])
        q = dot(a, wqkv[:, :width]) * factor
        k = dot(a, wqkv[:, width : 2 * width]).astype(BF16)
        v = dot(a, wqkv[:, 2 * width :]).astype(BF16)
        h1 = h + dot(feature_mix(q, k, v), wout[...])
        b = normed(h1, gains_ref[0, 1:2, :])
        query = (dot(b, wquery[...]) * factor).astype(BF16)

        @pl.when(first & (m == 0))
        def _():
            pass_cache()
            stack_cache()

        result = h1 + dot(item_mix(query), witem[...])
        h_out[m] = result.astype(BF16)

        @pl.when(sends)
        def _():
            h_copy(m, section + 1).start()

        staged[m] = result.reshape(feats, rows_n, gd, width).astype(BF16)
        out_copy(m, mine).start()
        out_own(m).start()
        return carry

    lax.fori_loop(0, micro, step, 0)

    for m in range(micro):
        out_own(m).wait()
        out_copy(m, theirs).wait()

    @pl.when(first)
    def _():
        for m in range(micro):
            x_copy(m, feat).wait_send()

    @pl.when(sends)
    def _():
        for m in range(micro):
            h_copy(m, section + 1).wait_send()

    for off in range(1, row_devs):
        cache_copy(off).wait_send()
    for off in range(row_devs):
        cache_pass(off, feat).wait_send()


def per_device(sizes, test_rows, train_cache, pattern, feat_qkv, feat_out, item_query, item_out, gains):
    sections, row_devs = sizes
    micro, test_n, gd, width = test_rows.shape
    train_dev = train_cache.shape[2]
    feats = 2
    rows_n = test_n // feats
    tokens = test_n * gd
    nk = row_devs * train_dev * gd
    pair_w = 2 * (width // HEADS)
    pairs = width // pair_w
    anywhere = pl.BlockSpec(memory_space=pl.ANY)
    vmem = pl.BlockSpec(memory_space=pltpu.VMEM)
    dma = pltpu.SemaphoreType.DMA
    return pl.pallas_call(
        functools.partial(kernel, sizes),
        out_shape=jax.ShapeDtypeStruct((1, micro, test_n, gd, width), BF16),
        in_specs=[anywhere, anywhere, vmem, anywhere, anywhere, anywhere, anywhere, vmem],
        out_specs=anywhere,
        scratch_shapes=[
            pltpu.VMEM((micro, feats, rows_n, gd, width), BF16),
            pltpu.VMEM((width, 3 * width), BF16),
            pltpu.VMEM((width, width), BF16),
            pltpu.VMEM((width, width), BF16),
            pltpu.VMEM((width, width), BF16),
            pltpu.VMEM((micro, tokens, width), BF16),
            pltpu.VMEM((micro, tokens, width), BF16),
            pltpu.VMEM((feats, row_devs, 2, train_dev, gd, width), BF16),
            pltpu.VMEM((feats, pairs, 2 * nk, pair_w), BF16),
            pltpu.VMEM((feats, pairs, 2 * nk, 2 * pair_w), BF16),
            pltpu.VMEM((2 * tokens, tokens), F32),
            pltpu.VMEM((tokens // feats, 2 * nk), F32),
            pltpu.VMEM((micro, feats, rows_n, gd, width), BF16),
            dma((4,)),
            dma((micro,)),
            dma(()),
            dma((micro,)),
            dma((micro,)),
            dma((micro,)),
            dma((row_devs - 1,)),
            dma((row_devs,)),
            dma((row_devs,)),
            dma((row_devs,)),
            dma((micro,)),
            dma((micro,)),
            dma((micro,)),
            dma((micro,)),
        ],
        compiler_params=pltpu.CompilerParams(
            collective_id=0, has_side_effects=True, vmem_limit_bytes=60 * 1024 * 1024
        ),
    )(test_rows, train_cache, pattern, feat_qkv, feat_out, item_query, item_out, gains)


def solution(mesh):
    sizes = (mesh.shape["section"], mesh.shape["rows"])
    return jax.shard_map(
        functools.partial(per_device, sizes),
        mesh=mesh,
        in_specs=(
            P(None, ("groups", "rows"), "feat", None),
            P("section", None, ("groups", "rows"), "feat", None),
            P(),
            P("section", None, None),
            P("section", None, None),
            P("section", None, None),
            P("section", None, None),
            P("section", None, None),
        ),
        out_specs=P("section", None, ("groups", "rows"), "feat", None),
        check_vma=False,
    )
```

```python
import functools
import math

import jax
import jax.numpy as jnp
from jax import lax
from jax.experimental import pallas as pl
from jax.experimental.pallas import tpu as pltpu
from jax.sharding import PartitionSpec as P

HEADS = 8
MESH = pl.DeviceIdType.MESH
F32 = jnp.float32
BF16 = jnp.bfloat16
EXCLUDED = -1e30


def iota(shape, dim):
    return lax.broadcasted_iota(jnp.int32, shape, dim)


def normed(x, gain):
    mean_sq = jnp.mean(x * x, axis=-1, keepdims=True)
    return (x * lax.rsqrt(mean_sq + 1e-06) * gain).astype(BF16)


def dot(a, b):
    return jnp.dot(a, b, preferred_element_type=F32)


def dot_t(a, b):
    return lax.dot_general(a, b, (((1,), (1,)), ((), ())), preferred_element_type=F32)


def kernel(
    sizes, rows_hbm, cache_hbm, pattern_ref, qkv_hbm, out_hbm, query_hbm, item_hbm, gains_ref, hidden_hbm,
    x_buf, wqkv, wout, wquery, witem, h_buf, h_out, h1_buf, query_buf, cache_buf, k_stack, v_stack, feat_bias, item_bias, staged,
    weight_sem, x_sem, own_sem, out_sem, x_send, x_recv, cache_send, cache_recv, pass_send, pass_recv,
    h_send, h_recv, out_send, out_recv,
):
    sections, row_devs = sizes
    micro, feats, rows_n, gd, width = x_buf.shape
    half = rows_n * gd
    tokens = feats * half
    pair_w = 2 * (width // HEADS)
    pairs = width // pair_w
    train_dev = cache_buf.shape[3]
    nk = row_devs * train_dev * gd
    factor = math.log2(math.e) / math.sqrt(width // HEADS)

    section = lax.axis_index("section")
    row = lax.axis_index("rows")
    feat = lax.axis_index("feat")
    partner = 1 - feat
    first = section == 0
    receives = section > 0
    sends = section < sections - 1
    mine = pl.ds(feat * rows_n, rows_n)
    theirs = pl.ds(partner * rows_n, rows_n)

    weights = [
        pltpu.make_async_copy(src.at[0], dst, weight_sem.at[i])
        for i, (src, dst) in enumerate(
            [(qkv_hbm, wqkv), (out_hbm, wout), (query_hbm, wquery), (item_hbm, witem)]
        )
    ]

    def x_own(m):
        return pltpu.make_async_copy(rows_hbm.at[m, mine], x_buf.at[m, feat], x_sem.at[m])

    @pl.when(first)
    def _():
        for m in range(micro):
            x_own(m).start()

    for copy in weights:
        copy.start()
    own_cache = pltpu.make_async_copy(cache_hbm.at[0], cache_buf.at[feat, row], own_sem)
    own_cache.start()

    barrier = pltpu.get_barrier_semaphore()
    pl.semaphore_signal(barrier, inc=1, device_id={"feat": partner}, device_id_type=MESH)
    for off in range(1, row_devs):
        pl.semaphore_signal(
            barrier, inc=1, device_id={"rows": lax.rem(row + off, row_devs)}, device_id_type=MESH
        )

    @pl.when(receives)
    def _():
        pl.semaphore_signal(barrier, inc=1, device_id={"section": section - 1}, device_id_type=MESH)

    @pl.when(sends)
    def _():
        pl.semaphore_signal(barrier, inc=1, device_id={"section": section + 1}, device_id_type=MESH)

    pl.semaphore_wait(
        barrier, row_devs + jnp.where(receives, 1, 0) + jnp.where(sends, 1, 0)
    )

    def x_copy(m, source):
        return pltpu.make_async_remote_copy(
            src_ref=rows_hbm.at[m, theirs], dst_ref=x_buf.at[m, source],
            send_sem=x_send.at[m], recv_sem=x_recv.at[m],
            device_id={"feat": partner}, device_id_type=MESH,
        )

    def cache_copy(off):
        return pltpu.make_async_remote_copy(
            src_ref=cache_hbm.at[0], dst_ref=cache_buf.at[feat, row],
            send_sem=cache_send.at[off - 1], recv_sem=cache_recv.at[row],
            device_id={"rows": lax.rem(row + off, row_devs)}, device_id_type=MESH,
        )

    def cache_arrival(off):
        source = lax.rem(row + off, row_devs)
        return pltpu.make_async_remote_copy(
            src_ref=cache_hbm.at[0], dst_ref=cache_buf.at[feat, source],
            send_sem=cache_send.at[off - 1], recv_sem=cache_recv.at[source],
            device_id={"rows": source}, device_id_type=MESH,
        )

    def cache_pass(off, source_feat):
        source = lax.rem(row + off, row_devs)
        return pltpu.make_async_remote_copy(
            src_ref=cache_hbm.at[0] if off == 0 else cache_buf.at[feat, source],
            dst_ref=cache_buf.at[source_feat, source],
            send_sem=pass_send.at[off], recv_sem=pass_recv.at[off],
            device_id={"feat": partner}, device_id_type=MESH,
        )

    @pl.when(first)
    def _():
        x_copy(0, feat).start()

    for off in range(1, row_devs):
        cache_copy(off).start()

    @pl.when(first)
    def _():
        for m in range(1, micro):
            x_copy(m, feat).start()

    cache_pass(0, feat).start()

    def h_copy(m, target):
        return pltpu.make_async_remote_copy(
            src_ref=h_out.at[m], dst_ref=h_buf.at[m],
            send_sem=h_send.at[m], recv_sem=h_recv.at[m],
            device_id={"section": target}, device_id_type=MESH,
        )

    def out_own(m):
        return pltpu.make_async_copy(staged.at[m, feat], hidden_hbm.at[0, m, mine], out_sem.at[m])

    def out_copy(m, place):
        return pltpu.make_async_remote_copy(
            src_ref=staged.at[m, partner], dst_ref=hidden_hbm.at[0, m, place],
            send_sem=out_send.at[m], recv_sem=out_recv.at[m],
            device_id={"feat": partner}, device_id_type=MESH,
        )

    groups = feats * gd
    token = iota((tokens, groups), 0)
    pick_q = ((token // half) * gd + token % gd == iota((tokens, groups), 1)).astype(F32)
    token = iota((groups, tokens), 1)
    pick_k = ((token // half) * gd + token % gd == iota((groups, tokens), 0)).astype(F32)
    pattern = (pattern_ref[...] != 0).astype(F32)
    seen = dot(dot(pick_q, pattern), pick_k) > 0.5
    qi, ki = iota((tokens, tokens), 0), iota((tokens, tokens), 1)
    seen = (seen | (qi == ki)) & ((qi % half) // gd == (ki % half) // gd)
    bias = jnp.where(seen, 0.0, EXCLUDED).astype(F32)
    feat_bias[:tokens] = bias
    feat_bias[tokens:] = bias
    item_bias[...] = jnp.where(
        iota((half, 2 * nk), 0) % gd == iota((half, 2 * nk), 1) % gd, 0.0, EXCLUDED
    ).astype(F32)

    def pass_cache():
        for off in range(1, row_devs):
            cache_arrival(off).wait_recv()
            cache_pass(off, feat).start()

    def stack_cache():
        own_cache.wait()
        for off in range(row_devs):
            cache_pass(off, partner).wait_recv()
        side = iota((nk, pair_w), 1) < pair_w // 2
        one = jnp.where(side, 1.0, 0.0).astype(BF16)
        other = jnp.where(side, 0.0, 1.0).astype(BF16)
        for f in range(feats):
            for pair in range(pairs):
                lanes = slice(pair * pair_w, (pair + 1) * pair_w)
                k = cache_buf[f, :, 0, :, :, lanes].astype(F32).reshape(nk, pair_w)
                v = cache_buf[f, :, 1, :, :, lanes].astype(F32).reshape(nk, pair_w)
                k_stack[f, pair, :nk] = jnp.where(side, k, 0.0).astype(BF16)
                k_stack[f, pair, nk:] = jnp.where(side, 0.0, k).astype(BF16)
                v_stack[f, pair, :nk, :pair_w] = jnp.where(side, v, 0.0).astype(BF16)
                v_stack[f, pair, nk:, :pair_w] = jnp.where(side, 0.0, v).astype(BF16)
                v_stack[f, pair, :nk, pair_w:] = one
                v_stack[f, pair, nk:, pair_w:] = other

    low_half = iota((tokens, pair_w), 1) < pair_w // 2
    ones = jnp.ones((tokens, pair_w), BF16)

    def feature_mix(q, k, v):
        mixed = []
        for pair in range(pairs):
            lanes = slice(pair * pair_w, (pair + 1) * pair_w)
            q1 = q[:, lanes]
            q2 = jnp.concatenate(
                [jnp.where(low_half, q1, 0.0).astype(BF16), jnp.where(low_half, 0.0, q1).astype(BF16)], axis=0
            )
            s = dot_t(q2, k[:, lanes]) + feat_bias[...]
            p = jnp.exp2(s - jnp.max(s, axis=-1, keepdims=True)).astype(BF16)
            o = dot(p, jnp.concatenate([v[:, lanes], ones], axis=1))
            total = jnp.where(low_half, o[:tokens, pair_w:], o[tokens:, pair_w:])
            o = jnp.where(low_half, o[:tokens, :pair_w], o[tokens:, :pair_w])
            mixed.append((o * pl.reciprocal(total, approx=True)).astype(BF16))
        return jnp.concatenate(mixed, axis=1)

    low_keys = iota((half, 2 * nk), 1) < nk

    def item_mix(query):
        blocks = []
        for f in range(feats):
            mixed = []
            for pair in range(pairs):
                lanes = slice(pair * pair_w, (pair + 1) * pair_w)
                s = dot_t(query[f * half : (f + 1) * half, lanes], k_stack[f, pair]) + item_bias[...]
                low = jnp.max(jnp.where(low_keys, s, -jnp.inf), axis=-1, keepdims=True)
                high = jnp.max(jnp.where(low_keys, -jnp.inf, s), axis=-1, keepdims=True)
                p = jnp.exp2(s - jnp.where(low_keys, low, high)).astype(BF16)
                o = dot(p, v_stack[f, pair])
                mixed.append((o[:, :pair_w] * pl.reciprocal(o[:, pair_w:], approx=True)).astype(BF16))
            blocks.append(jnp.concatenate(mixed, axis=1))
        return jnp.concatenate(blocks, axis=0)

    @pl.when(receives)
    def _():
        pass_cache()
        stack_cache()

    for copy in weights:
        copy.wait()

    def feature_half(places):
        count = len(places) * tokens
        h = jnp.concatenate([h_buf[m] for m in places], axis=0).astype(F32)
        a = normed(h, gains_ref[0, 0:1, :])
        q = dot(a, wqkv[:, :width]) * factor
        k = dot(a, wqkv[:, width : 2 * width]).astype(BF16)
        v = dot(a, wqkv[:, 2 * width :]).astype(BF16)
        spans = [slice(at, at + tokens) for at in range(0, count, tokens)]
        mixed = jnp.concatenate([feature_mix(q[at], k[at], v[at]) for at in spans], axis=0)
        h1 = h + dot(mixed, wout[...])
        b = normed(h1, gains_ref[0, 1:2, :])
        query = (dot(b, wquery[...]) * factor).astype(BF16)
        for m, at in zip(places, spans):
            h1_buf[m] = h1[at]
            query_buf[m] = query[at]

    @pl.when(first)
    def _():
        for m in range(micro):
            x_own(m).wait()
            x_copy(m, partner).wait_recv()
            h_buf[m] = x_buf[m].astype(F32).reshape(tokens, width).astype(BF16)
        pass_cache()
        feature_half(range(micro))
        stack_cache()

    def step(m, carry):
        @pl.when(receives)
        def _():
            h_copy(m, section - 1).wait_recv()
            feature_half([m])

        result = h1_buf[m] + dot(item_mix(query_buf[m]), witem[...])
        h_out[m] = result.astype(BF16)

        @pl.when(sends)
        def _():
            h_copy(m, section + 1).start()

        staged[m] = result.reshape(feats, rows_n, gd, width).astype(BF16)
        out_copy(m, mine).start()
        out_own(m).start()
        return carry

    lax.fori_loop(0, micro, step, 0)

    for m in range(micro):
        out_own(m).wait()
        out_copy(m, theirs).wait()

    @pl.when(first)
    def _():
        for m in range(micro):
            x_copy(m, feat).wait_send()

    @pl.when(sends)
    def _():
        for m in range(micro):
            h_copy(m, section + 1).wait_send()

    for off in range(1, row_devs):
        cache_copy(off).wait_send()
    for off in range(row_devs):
        cache_pass(off, feat).wait_send()


def hand_over(source, target, sem):
    copies = [
        pltpu.make_async_copy(source.at[0, m], target.at[0, m], sem.at[m])
        for m in range(source.shape[1])
    ]
    for copy in copies:
        copy.start()
    for copy in copies:
        copy.wait()


def per_device(sizes, test_rows, train_cache, pattern, feat_qkv, feat_out, item_query, item_out, gains):
    sections, row_devs = sizes
    micro, test_n, gd, width = test_rows.shape
    train_dev = train_cache.shape[2]
    feats = 2
    rows_n = test_n // feats
    tokens = test_n * gd
    nk = row_devs * train_dev * gd
    pair_w = 2 * (width // HEADS)
    pairs = width // pair_w
    anywhere = pl.BlockSpec(memory_space=pl.ANY)
    vmem = pl.BlockSpec(memory_space=pltpu.VMEM)
    dma = pltpu.SemaphoreType.DMA
    hidden = pl.pallas_call(
        functools.partial(kernel, sizes),
        out_shape=jax.ShapeDtypeStruct((1, micro, test_n, gd, width), BF16),
        in_specs=[anywhere, anywhere, vmem, anywhere, anywhere, anywhere, anywhere, vmem],
        out_specs=anywhere,
        scratch_shapes=[
            pltpu.VMEM((micro, feats, rows_n, gd, width), BF16),
            pltpu.VMEM((width, 3 * width), BF16),
            pltpu.VMEM((width, width), BF16),
            pltpu.VMEM((width, width), BF16),
            pltpu.VMEM((width, width), BF16),
            pltpu.VMEM((micro, tokens, width), BF16),
            pltpu.VMEM((micro, tokens, width), BF16),
            pltpu.VMEM((micro, tokens, width), F32),
            pltpu.VMEM((micro, tokens, width), BF16),
            pltpu.VMEM((feats, row_devs, 2, train_dev, gd, width), BF16),
            pltpu.VMEM((feats, pairs, 2 * nk, pair_w), BF16),
            pltpu.VMEM((feats, pairs, 2 * nk, 2 * pair_w), BF16),
            pltpu.VMEM((2 * tokens, tokens), F32),
            pltpu.VMEM((tokens // feats, 2 * nk), F32),
            pltpu.VMEM((micro, feats, rows_n, gd, width), BF16),
            dma((4,)),
            dma((micro,)),
            dma(()),
            dma((micro,)),
            dma((micro,)),
            dma((micro,)),
            dma((row_devs - 1,)),
            dma((row_devs,)),
            dma((row_devs,)),
            dma((row_devs,)),
            dma((micro,)),
            dma((micro,)),
            dma((micro,)),
            dma((micro,)),
        ],
        compiler_params=pltpu.CompilerParams(
            collective_id=0, has_side_effects=True, vmem_limit_bytes=60 * 1024 * 1024
        ),
    )(test_rows, train_cache, pattern, feat_qkv, feat_out, item_query, item_out, gains)
    return pl.pallas_call(
        hand_over,
        out_shape=jax.ShapeDtypeStruct(hidden.shape, hidden.dtype),
        in_specs=[anywhere],
        out_specs=anywhere,
        scratch_shapes=[dma((micro,))],
    )(hidden)


def solution(mesh):
    sizes = (mesh.shape["section"], mesh.shape["rows"])
    return jax.shard_map(
        functools.partial(per_device, sizes),
        mesh=mesh,
        in_specs=(
            P(None, ("groups", "rows"), "feat", None),
            P("section", None, ("groups", "rows"), "feat", None),
            P(),
            P("section", None, None),
            P("section", None, None),
            P("section", None, None),
            P("section", None, None),
            P("section", None, None),
        ),
        out_specs=P("section", None, ("groups", "rows"), "feat", None),
        check_vma=False,
    )
```

```python
import functools
import math

import jax
import jax.numpy as jnp
from jax import lax
from jax.experimental import pallas as pl
from jax.experimental.pallas import tpu as pltpu
from jax.sharding import PartitionSpec as P

HEADS = 8
MESH = pl.DeviceIdType.MESH
F32 = jnp.float32
BF16 = jnp.bfloat16
EXCLUDED = -1e30


def iota(shape, dim):
    return lax.broadcasted_iota(jnp.int32, shape, dim)


def normed(x, gain):
    mean_sq = jnp.mean(x * x, axis=-1, keepdims=True)
    return (x * lax.rsqrt(mean_sq + 1e-06) * gain).astype(BF16)


def dot(a, b):
    return jnp.dot(a, b, preferred_element_type=F32)


def dot_t(a, b):
    return lax.dot_general(a, b, (((1,), (1,)), ((), ())), preferred_element_type=F32)


def kernel(
    sizes, rows_hbm, cache_hbm, pattern_ref, qkv_hbm, out_hbm, query_hbm, item_hbm, gains_ref, hidden_hbm,
    x_buf, wqkv, wout, wquery, witem, h_buf, h_out, cache_buf, k_stack, v_stack, feat_bias, item_bias, staged, wide, cache_wide,
    weight_sem, x_sem, own_sem, out_sem, x_send, x_recv, cache_send, cache_recv, pass_send, pass_recv,
    h_send, h_recv, out_send, out_recv,
):
    sections, row_devs = sizes
    micro, tokens, width = h_buf.shape
    feats = x_buf.shape[1]
    pair_w = 2 * (width // HEADS)
    pairs = width // pair_w
    half = tokens // feats
    gd = pattern_ref.shape[0] // feats
    rows_n = half // gd
    per_row = gd * pairs
    train_n = cache_wide.shape[0] // per_row
    nk = train_n * gd
    factor = math.log2(math.e) / math.sqrt(width // HEADS)

    section = lax.axis_index("section")
    row = lax.axis_index("rows")
    feat = lax.axis_index("feat")
    partner = 1 - feat
    first = section == 0
    receives = section > 0
    sends = section < sections - 1
    block_n = rows_n * per_row
    mine = pl.ds(feat * block_n, block_n)
    theirs = pl.ds(partner * block_n, block_n)

    weights = [
        pltpu.make_async_copy(src.at[0], dst, weight_sem.at[i])
        for i, (src, dst) in enumerate(
            [(qkv_hbm, wqkv), (out_hbm, wout), (query_hbm, wquery), (item_hbm, witem)]
        )
    ]

    def x_own(m):
        return pltpu.make_async_copy(rows_hbm.at[m, mine], x_buf.at[m, feat], x_sem.at[m])

    @pl.when(first)
    def _():
        for m in range(micro):
            x_own(m).start()

    for copy in weights:
        copy.start()
    own_cache = pltpu.make_async_copy(cache_hbm.at[0], cache_buf.at[feat, row], own_sem)
    own_cache.start()

    barrier = pltpu.get_barrier_semaphore()
    pl.semaphore_signal(barrier, inc=1, device_id={"feat": partner}, device_id_type=MESH)
    for off in range(1, row_devs):
        pl.semaphore_signal(
            barrier, inc=1, device_id={"rows": lax.rem(row + off, row_devs)}, device_id_type=MESH
        )

    @pl.when(receives)
    def _():
        pl.semaphore_signal(barrier, inc=1, device_id={"section": section - 1}, device_id_type=MESH)

    @pl.when(sends)
    def _():
        pl.semaphore_signal(barrier, inc=1, device_id={"section": section + 1}, device_id_type=MESH)

    pl.semaphore_wait(
        barrier, row_devs + jnp.where(receives, 1, 0) + jnp.where(sends, 1, 0)
    )

    def x_copy(m, source):
        return pltpu.make_async_remote_copy(
            src_ref=rows_hbm.at[m, theirs], dst_ref=x_buf.at[m, source],
            send_sem=x_send.at[m], recv_sem=x_recv.at[m],
            device_id={"feat": partner}, device_id_type=MESH,
        )

    def cache_copy(off):
        return pltpu.make_async_remote_copy(
            src_ref=cache_hbm.at[0], dst_ref=cache_buf.at[feat, row],
            send_sem=cache_send.at[off - 1], recv_sem=cache_recv.at[row],
            device_id={"rows": lax.rem(row + off, row_devs)}, device_id_type=MESH,
        )

    def cache_arrival(off):
        source = lax.rem(row + off, row_devs)
        return pltpu.make_async_remote_copy(
            src_ref=cache_hbm.at[0], dst_ref=cache_buf.at[feat, source],
            send_sem=cache_send.at[off - 1], recv_sem=cache_recv.at[source],
            device_id={"rows": source}, device_id_type=MESH,
        )

    def cache_pass(off, source_feat):
        source = lax.rem(row + off, row_devs)
        return pltpu.make_async_remote_copy(
            src_ref=cache_hbm.at[0] if off == 0 else cache_buf.at[feat, source],
            dst_ref=cache_buf.at[source_feat, source],
            send_sem=pass_send.at[off], recv_sem=pass_recv.at[off],
            device_id={"feat": partner}, device_id_type=MESH,
        )

    @pl.when(first)
    def _():
        x_copy(0, feat).start()

    for off in range(1, row_devs):
        cache_copy(off).start()

    @pl.when(first)
    def _():
        for m in range(1, micro):
            x_copy(m, feat).start()

    cache_pass(0, feat).start()

    def h_copy(m, target):
        return pltpu.make_async_remote_copy(
            src_ref=h_out.at[m], dst_ref=h_buf.at[m],
            send_sem=h_send.at[m], recv_sem=h_recv.at[m],
            device_id={"section": target}, device_id_type=MESH,
        )

    def out_own(m):
        return pltpu.make_async_copy(staged.at[m, feat], hidden_hbm.at[0, m, mine], out_sem.at[m])

    def out_copy(m, place):
        return pltpu.make_async_remote_copy(
            src_ref=staged.at[m, partner], dst_ref=hidden_hbm.at[0, m, place],
            send_sem=out_send.at[m], recv_sem=out_recv.at[m],
            device_id={"feat": partner}, device_id_type=MESH,
        )

    groups = feats * gd
    pick_q = (iota((tokens, groups), 0) // rows_n == iota((tokens, groups), 1)).astype(F32)
    pick_k = (iota((groups, tokens), 1) // rows_n == iota((groups, tokens), 0)).astype(F32)
    pattern = (pattern_ref[...] != 0).astype(F32)
    seen = dot(dot(pick_q, pattern), pick_k) > 0.5
    qi, ki = iota((tokens, tokens), 0), iota((tokens, tokens), 1)
    seen = (seen | (qi == ki)) & (qi % rows_n == ki % rows_n)
    bias = jnp.where(seen, 0.0, EXCLUDED).astype(F32)
    feat_bias[:tokens] = bias
    feat_bias[tokens:] = bias
    item_bias[...] = jnp.where(
        iota((half, 2 * nk), 0) // rows_n == (iota((half, 2 * nk), 1) % nk) // train_n, 0.0, EXCLUDED
    ).astype(F32)

    def pass_cache():
        for off in range(1, row_devs):
            cache_arrival(off).wait_recv()
            cache_pass(off, feat).start()

    def stack_cache():
        own_cache.wait()
        for off in range(row_devs):
            cache_pass(off, partner).wait_recv()
        side = iota((nk, pair_w), 1) < pair_w // 2
        one = jnp.where(side, 1.0, 0.0).astype(BF16)
        other = jnp.where(side, 0.0, 1.0).astype(BF16)
        for f in range(feats):
            for kind in range(2):
                cache_wide[...] = cache_buf[f, :, kind].astype(F32).reshape(cache_wide.shape)
                for pair in range(pairs):
                    part = jnp.concatenate(
                        [cache_wide[pl.ds(pair * gd + g, train_n, stride=per_row), :] for g in range(gd)], axis=0
                    )
                    low = jnp.where(side, part, 0.0).astype(BF16)
                    high = jnp.where(side, 0.0, part).astype(BF16)
                    if kind == 0:
                        k_stack[f, pair, :nk] = low
                        k_stack[f, pair, nk:] = high
                    else:
                        v_stack[f, pair, :nk, :pair_w] = low
                        v_stack[f, pair, nk:, :pair_w] = high
                        v_stack[f, pair, :nk, pair_w:] = one
                        v_stack[f, pair, nk:, pair_w:] = other

    low_half = iota((tokens, pair_w), 1) < pair_w // 2
    ones = jnp.ones((tokens, pair_w), BF16)

    def feature_mix(q, k, v):
        mixed = []
        for pair in range(pairs):
            lanes = slice(pair * pair_w, (pair + 1) * pair_w)
            q1 = q[:, lanes]
            q2 = jnp.concatenate(
                [jnp.where(low_half, q1, 0.0).astype(BF16), jnp.where(low_half, 0.0, q1).astype(BF16)], axis=0
            )
            s = dot_t(q2, k[:, lanes]) + feat_bias[...]
            p = jnp.exp2(s - jnp.max(s, axis=-1, keepdims=True)).astype(BF16)
            o = dot(p, jnp.concatenate([v[:, lanes], ones], axis=1))
            total = jnp.where(low_half, o[:tokens, pair_w:], o[tokens:, pair_w:])
            o = jnp.where(low_half, o[:tokens, :pair_w], o[tokens:, :pair_w])
            mixed.append((o * pl.reciprocal(total, approx=True)).astype(BF16))
        return jnp.concatenate(mixed, axis=1)

    low_keys = iota((half, 2 * nk), 1) < nk

    def item_mix(query):
        blocks = []
        for f in range(feats):
            mixed = []
            for pair in range(pairs):
                lanes = slice(pair * pair_w, (pair + 1) * pair_w)
                s = dot_t(query[f * half : (f + 1) * half, lanes], k_stack[f, pair]) + item_bias[...]
                low = jnp.max(jnp.where(low_keys, s, -jnp.inf), axis=-1, keepdims=True)
                high = jnp.max(jnp.where(low_keys, -jnp.inf, s), axis=-1, keepdims=True)
                p = jnp.exp2(s - jnp.where(low_keys, low, high)).astype(BF16)
                o = dot(p, v_stack[f, pair])
                mixed.append((o[:, :pair_w] * pl.reciprocal(o[:, pair_w:], approx=True)).astype(BF16))
            blocks.append(jnp.concatenate(mixed, axis=1))
        return jnp.concatenate(blocks, axis=0)

    @pl.when(receives)
    def _():
        pass_cache()
        stack_cache()

    weights[0].wait()
    weights[1].wait()
    weights[2].wait()
    weights[3].wait()

    def spread(pair):
        return [
            pl.ds(f * block_n + pair * gd + g, rows_n, stride=per_row)
            for f in range(feats)
            for g in range(gd)
        ]

    def step(m, carry):
        @pl.when(first)
        def _():
            x_own(m).wait()
            x_copy(m, partner).wait_recv()
            wide[...] = x_buf[m].astype(F32).reshape(wide.shape)
            for pair in range(pairs):
                part = [wide[place, :] for place in spread(pair)]
                lanes = slice(pair * pair_w, (pair + 1) * pair_w)
                h_buf[m, :, lanes] = jnp.concatenate(part, axis=0).astype(BF16)

        @pl.when(receives)
        def _():
            h_copy(m, section - 1).wait_recv()

        h = h_buf[m].astype(F32)
        a = normed(h, gains_ref[0, 0:1, :])
        q = dot(a, wqkv[:, :width]) * factor
        k = dot(a, wqkv[:, width : 2 * width]).astype(BF16)
        v = dot(a, wqkv[:, 2 * width :]).astype(BF16)
        h1 = h + dot(feature_mix(q, k, v), wout[...])
        b = normed(h1, gains_ref[0, 1:2, :])
        query = (dot(b, wquery[...]) * factor).astype(BF16)

        @pl.when(first & (m == 0))
        def _():
            pass_cache()
            stack_cache()

        result = h1 + dot(item_mix(query), witem[...])
        h_out[m] = result.astype(BF16)

        @pl.when(sends)
        def _():
            h_copy(m, section + 1).start()

        for pair in range(pairs):
            for at, place in enumerate(spread(pair)):
                wide[place, :] = result[at * rows_n : (at + 1) * rows_n, pair * pair_w : (pair + 1) * pair_w]
        staged[m] = wide[...].reshape(feats, block_n, pair_w).astype(BF16)
        out_copy(m, mine).start()
        out_own(m).start()
        return carry

    lax.fori_loop(0, micro, step, 0)

    for m in range(micro):
        out_own(m).wait()
        out_copy(m, theirs).wait()

    @pl.when(first)
    def _():
        for m in range(micro):
            x_copy(m, feat).wait_send()

    @pl.when(sends)
    def _():
        for m in range(micro):
            h_copy(m, section + 1).wait_send()

    for off in range(1, row_devs):
        cache_copy(off).wait_send()
    for off in range(row_devs):
        cache_pass(off, feat).wait_send()


def hand_over(source, target, sem):
    micro, parts = sem.shape
    piece = source.shape[2] // parts
    copies = []
    for m in range(micro):
        for part in range(parts):
            span = pl.ds(part * piece, piece)
            copies.append(
                pltpu.make_async_copy(source.at[0, m, span], target.at[0, m, span], sem.at[m, part])
            )
    for copy in copies:
        copy.start()
    for copy in copies:
        copy.wait()


def per_device(sizes, test_rows, train_cache, pattern, feat_qkv, feat_out, item_query, item_out, gains):
    sections, row_devs = sizes
    micro, test_n, gd, width = test_rows.shape
    train_dev = train_cache.shape[2]
    feats = 2
    rows_n = test_n // feats
    tokens = test_n * gd
    nk = row_devs * train_dev * gd
    pair_w = 2 * (width // HEADS)
    pairs = width // pair_w
    anywhere = pl.BlockSpec(memory_space=pl.ANY)
    vmem = pl.BlockSpec(memory_space=pltpu.VMEM)
    dma = pltpu.SemaphoreType.DMA
    per_row = gd * pairs

    def as_rows(x):
        pieces = x.reshape(x.shape[:-1] + (pairs, pair_w)).swapaxes(-3, -2)
        return pieces.reshape(x.shape[:-3] + (x.shape[-3] * per_row, pair_w))

    hidden = pl.pallas_call(
        functools.partial(kernel, sizes),
        out_shape=jax.ShapeDtypeStruct((1, micro, test_n * per_row, pair_w), BF16),
        in_specs=[anywhere, anywhere, vmem, anywhere, anywhere, anywhere, anywhere, vmem],
        out_specs=anywhere,
        scratch_shapes=[
            pltpu.VMEM((micro, feats, rows_n * per_row, pair_w), BF16),
            pltpu.VMEM((width, 3 * width), BF16),
            pltpu.VMEM((width, width), BF16),
            pltpu.VMEM((width, width), BF16),
            pltpu.VMEM((width, width), BF16),
            pltpu.VMEM((micro, tokens, width), BF16),
            pltpu.VMEM((micro, tokens, width), BF16),
            pltpu.VMEM((feats, row_devs, 2, train_dev * per_row, pair_w), BF16),
            pltpu.VMEM((feats, pairs, 2 * nk, pair_w), BF16),
            pltpu.VMEM((feats, pairs, 2 * nk, 2 * pair_w), BF16),
            pltpu.VMEM((2 * tokens, tokens), F32),
            pltpu.VMEM((tokens // feats, 2 * nk), F32),
            pltpu.VMEM((micro, feats, rows_n * per_row, pair_w), BF16),
            pltpu.VMEM((test_n * per_row, pair_w), F32),
            pltpu.VMEM((row_devs * train_dev * per_row, pair_w), F32),
            dma((4,)),
            dma((micro,)),
            dma(()),
            dma((micro,)),
            dma((micro,)),
            dma((micro,)),
            dma((row_devs - 1,)),
            dma((row_devs,)),
            dma((row_devs,)),
            dma((row_devs,)),
            dma((micro,)),
            dma((micro,)),
            dma((micro,)),
            dma((micro,)),
        ],
        compiler_params=pltpu.CompilerParams(
            collective_id=0, has_side_effects=True, vmem_limit_bytes=60 * 1024 * 1024
        ),
    )(as_rows(test_rows), as_rows(train_cache), pattern, feat_qkv, feat_out, item_query, item_out, gains)
    hidden = pl.pallas_call(
        hand_over,
        out_shape=jax.ShapeDtypeStruct(hidden.shape, hidden.dtype),
        in_specs=[anywhere],
        out_specs=anywhere,
        scratch_shapes=[dma((micro, 4))],
        compiler_params=pltpu.CompilerParams(vmem_limit_bytes=60 * 1024 * 1024),
    )(hidden)
    hidden = hidden.reshape(1, micro, test_n, pairs, gd, pair_w).swapaxes(-3, -2)
    return hidden.reshape(1, micro, test_n, gd, width)


def solution(mesh):
    sizes = (mesh.shape["section"], mesh.shape["rows"])
    return jax.shard_map(
        functools.partial(per_device, sizes),
        mesh=mesh,
        in_specs=(
            P(None, ("groups", "rows"), "feat", None),
            P("section", None, ("groups", "rows"), "feat", None),
            P(),
            P("section", None, None),
            P("section", None, None),
            P("section", None, None),
            P("section", None, None),
            P("section", None, None),
        ),
        out_specs=P("section", None, ("groups", "rows"), "feat", None),
        check_vma=False,
    )
```

```python
import functools
import math

import jax
import jax.numpy as jnp
from jax import lax
from jax.experimental import pallas as pl
from jax.experimental.pallas import tpu as pltpu
from jax.sharding import PartitionSpec as P

HEADS = 8
MESH = pl.DeviceIdType.MESH
F32 = jnp.float32
BF16 = jnp.bfloat16
EXCLUDED = -1e30


def iota(shape, dim):
    return lax.broadcasted_iota(jnp.int32, shape, dim)


def normed(x, gain):
    mean_sq = jnp.mean(x * x, axis=-1, keepdims=True)
    return (x * lax.rsqrt(mean_sq + 1e-06) * gain).astype(BF16)


def dot(a, b):
    return jnp.dot(a, b, preferred_element_type=F32)


def dot_t(a, b):
    return lax.dot_general(a, b, (((1,), (1,)), ((), ())), preferred_element_type=F32)


def kernel(
    sizes, rows_hbm, cache_hbm, pattern_ref, qkv_hbm, out_hbm, query_hbm, item_hbm, gains_ref, hidden_hbm,
    x_buf, wqkv, wout, wquery, witem, h_buf, h_out, cache_buf, k_stack, v_stack, feat_bias, item_bias, staged, wide, cache_wide, qkv, mix, query, h1_buf,
    weight_sem, x_sem, own_sem, out_sem, x_send, x_recv, cache_send, cache_recv, pass_send, pass_recv,
    h_send, h_recv, out_send, out_recv,
):
    sections, row_devs = sizes
    micro, tokens, width = h_buf.shape
    feats = x_buf.shape[1]
    pair_w = 2 * (width // HEADS)
    pairs = width // pair_w
    half = tokens // feats
    gd = pattern_ref.shape[0] // feats
    rows_n = half // gd
    per_row = gd * pairs
    train_n = cache_wide.shape[0] // per_row
    nk = train_n * gd
    factor = math.log2(math.e) / math.sqrt(width // HEADS)

    section = lax.axis_index("section")
    row = lax.axis_index("rows")
    feat = lax.axis_index("feat")
    partner = 1 - feat
    first = section == 0
    receives = section > 0
    sends = section < sections - 1
    block_n = rows_n * per_row
    mine = pl.ds(feat * block_n, block_n)
    theirs = pl.ds(partner * block_n, block_n)

    weights = [
        pltpu.make_async_copy(src.at[0], dst, weight_sem.at[i])
        for i, (src, dst) in enumerate(
            [(qkv_hbm, wqkv), (out_hbm, wout), (query_hbm, wquery), (item_hbm, witem)]
        )
    ]

    def x_own(m):
        return pltpu.make_async_copy(rows_hbm.at[m, mine], x_buf.at[m, feat], x_sem.at[m])

    @pl.when(first)
    def _():
        for m in range(micro):
            x_own(m).start()

    for copy in weights:
        copy.start()
    own_cache = pltpu.make_async_copy(cache_hbm.at[0], cache_buf.at[feat, row], own_sem)
    own_cache.start()

    barrier = pltpu.get_barrier_semaphore()
    pl.semaphore_signal(barrier, inc=1, device_id={"feat": partner}, device_id_type=MESH)
    for off in range(1, row_devs):
        pl.semaphore_signal(
            barrier, inc=1, device_id={"rows": lax.rem(row + off, row_devs)}, device_id_type=MESH
        )

    @pl.when(receives)
    def _():
        pl.semaphore_signal(barrier, inc=1, device_id={"section": section - 1}, device_id_type=MESH)

    @pl.when(sends)
    def _():
        pl.semaphore_signal(barrier, inc=1, device_id={"section": section + 1}, device_id_type=MESH)

    pl.semaphore_wait(
        barrier, row_devs + jnp.where(receives, 1, 0) + jnp.where(sends, 1, 0)
    )

    def x_copy(m, source):
        return pltpu.make_async_remote_copy(
            src_ref=rows_hbm.at[m, theirs], dst_ref=x_buf.at[m, source],
            send_sem=x_send.at[m], recv_sem=x_recv.at[m],
            device_id={"feat": partner}, device_id_type=MESH,
        )

    def cache_copy(off):
        return pltpu.make_async_remote_copy(
            src_ref=cache_hbm.at[0], dst_ref=cache_buf.at[feat, row],
            send_sem=cache_send.at[off - 1], recv_sem=cache_recv.at[row],
            device_id={"rows": lax.rem(row + off, row_devs)}, device_id_type=MESH,
        )

    def cache_arrival(off):
        source = lax.rem(row + off, row_devs)
        return pltpu.make_async_remote_copy(
            src_ref=cache_hbm.at[0], dst_ref=cache_buf.at[feat, source],
            send_sem=cache_send.at[off - 1], recv_sem=cache_recv.at[source],
            device_id={"rows": source}, device_id_type=MESH,
        )

    def cache_pass(off, source_feat):
        source = lax.rem(row + off, row_devs)
        return pltpu.make_async_remote_copy(
            src_ref=cache_hbm.at[0] if off == 0 else cache_buf.at[feat, source],
            dst_ref=cache_buf.at[source_feat, source],
            send_sem=pass_send.at[off], recv_sem=pass_recv.at[off],
            device_id={"feat": partner}, device_id_type=MESH,
        )

    @pl.when(first)
    def _():
        x_copy(0, feat).start()

    for off in range(1, row_devs):
        cache_copy(off).start()

    @pl.when(first)
    def _():
        for m in range(1, micro):
            x_copy(m, feat).start()

    cache_pass(0, feat).start()

    def h_copy(m, target):
        return pltpu.make_async_remote_copy(
            src_ref=h_out.at[m], dst_ref=h_buf.at[m],
            send_sem=h_send.at[m], recv_sem=h_recv.at[m],
            device_id={"section": target}, device_id_type=MESH,
        )

    def out_own(m):
        return pltpu.make_async_copy(staged.at[m, feat], hidden_hbm.at[0, m, mine], out_sem.at[m])

    def out_copy(m, place):
        return pltpu.make_async_remote_copy(
            src_ref=staged.at[m, partner], dst_ref=hidden_hbm.at[0, m, place],
            send_sem=out_send.at[m], recv_sem=out_recv.at[m],
            device_id={"feat": partner}, device_id_type=MESH,
        )

    groups = feats * gd
    pick_q = (iota((tokens, groups), 0) // rows_n == iota((tokens, groups), 1)).astype(F32)
    pick_k = (iota((groups, tokens), 1) // rows_n == iota((groups, tokens), 0)).astype(F32)
    pattern = (pattern_ref[...] != 0).astype(F32)
    seen = dot(dot(pick_q, pattern), pick_k) > 0.5
    qi, ki = iota((tokens, tokens), 0), iota((tokens, tokens), 1)
    seen = (seen | (qi == ki)) & (qi % rows_n == ki % rows_n)
    bias = jnp.where(seen, 0.0, EXCLUDED).astype(F32)
    feat_bias[:tokens] = bias
    feat_bias[tokens:] = bias
    item_bias[...] = jnp.where(
        iota((half, 2 * nk), 0) // rows_n == (iota((half, 2 * nk), 1) % nk) // train_n, 0.0, EXCLUDED
    ).astype(F32)

    def pass_cache():
        for off in range(1, row_devs):
            cache_arrival(off).wait_recv()
            cache_pass(off, feat).start()

    def stack_cache():
        own_cache.wait()
        for off in range(row_devs):
            cache_pass(off, partner).wait_recv()
        side = iota((nk, pair_w), 1) < pair_w // 2
        one = jnp.where(side, 1.0, 0.0).astype(BF16)
        other = jnp.where(side, 0.0, 1.0).astype(BF16)
        def one_kind(f, kind, store):
            cache_wide[...] = cache_buf[f, :, kind].astype(F32).reshape(cache_wide.shape)
            for pair in range(pairs):
                part = jnp.concatenate(
                    [cache_wide[pl.ds(pair * gd + g, train_n, stride=per_row), :] for g in range(gd)], axis=0
                )
                store(pair, jnp.where(side, part, 0.0).astype(BF16), jnp.where(side, 0.0, part).astype(BF16))

        def one_feat(f, carry):
            def keys(pair, low, high):
                k_stack[f, pair, :nk] = low
                k_stack[f, pair, nk:] = high

            def values(pair, low, high):
                v_stack[f, pair, :nk, :pair_w] = low
                v_stack[f, pair, nk:, :pair_w] = high
                v_stack[f, pair, :nk, pair_w:] = one
                v_stack[f, pair, nk:, pair_w:] = other

            one_kind(f, 0, keys)
            one_kind(f, 1, values)
            return carry

        lax.fori_loop(0, feats, one_feat, 0)

    low_half = iota((tokens, pair_w), 1) < pair_w // 2
    ones = jnp.ones((tokens, pair_w), BF16)

    def lanes_of(pair, offset=0):
        return pl.ds(pl.multiple_of(offset + pair * pair_w, pair_w), pair_w)

    def feature_mix():
        def one_pair(pair, carry):
            q1 = qkv[:, lanes_of(pair)] * factor
            k = qkv[:, lanes_of(pair, width)].astype(BF16)
            v = qkv[:, lanes_of(pair, 2 * width)].astype(BF16)
            q2 = jnp.concatenate(
                [jnp.where(low_half, q1, 0.0).astype(BF16), jnp.where(low_half, 0.0, q1).astype(BF16)], axis=0
            )
            s = dot_t(q2, k) + feat_bias[...]
            p = jnp.exp2(s - jnp.max(s, axis=-1, keepdims=True)).astype(BF16)
            o = dot(p, jnp.concatenate([v, ones], axis=1))
            total = jnp.where(low_half, o[:tokens, pair_w:], o[tokens:, pair_w:])
            o = jnp.where(low_half, o[:tokens, :pair_w], o[tokens:, :pair_w])
            mix[:, lanes_of(pair)] = (o * pl.reciprocal(total, approx=True)).astype(BF16)
            return carry

        lax.fori_loop(0, pairs, one_pair, 0)

    low_keys = iota((half, 2 * nk), 1) < nk

    def item_mix():
        def one_pair(pair, carry):
            for f in range(feats):
                span = slice(f * half, (f + 1) * half)
                s = dot_t(query[span, lanes_of(pair)], k_stack[f, pair]) + item_bias[...]
                low = jnp.max(jnp.where(low_keys, s, -jnp.inf), axis=-1, keepdims=True)
                high = jnp.max(jnp.where(low_keys, -jnp.inf, s), axis=-1, keepdims=True)
                p = jnp.exp2(s - jnp.where(low_keys, low, high)).astype(BF16)
                o = dot(p, v_stack[f, pair])
                mix[span, lanes_of(pair)] = (o[:, :pair_w] * pl.reciprocal(o[:, pair_w:], approx=True)).astype(BF16)
            return carry

        lax.fori_loop(0, pairs, one_pair, 0)

    @pl.when(receives)
    def _():
        pass_cache()
        stack_cache()

    weights[0].wait()
    weights[1].wait()
    weights[2].wait()
    weights[3].wait()

    def spread(pair):
        return [
            pl.ds(f * block_n + pair * gd + g, rows_n, stride=per_row)
            for f in range(feats)
            for g in range(gd)
        ]

    def step(m, carry):
        @pl.when(first)
        def _():
            x_own(m).wait()
            x_copy(m, partner).wait_recv()
            wide[...] = x_buf[m].astype(F32).reshape(wide.shape)
            for pair in range(pairs):
                part = [wide[place, :] for place in spread(pair)]
                lanes = slice(pair * pair_w, (pair + 1) * pair_w)
                h_buf[m, :, lanes] = jnp.concatenate(part, axis=0).astype(BF16)

        @pl.when(receives)
        def _():
            h_copy(m, section - 1).wait_recv()

        h = h_buf[m].astype(F32)
        a = normed(h, gains_ref[0, 0:1, :])
        def project(part, carry):
            columns = pl.ds(pl.multiple_of(part * width, width), width)
            qkv[:, columns] = dot(a, wqkv[:, columns])
            return carry

        lax.fori_loop(0, 3, project, 0)
        feature_mix()
        h1 = h + dot(mix[...], wout[...])
        h1_buf[...] = h1
        b = normed(h1, gains_ref[0, 1:2, :])
        query[...] = (dot(b, wquery[...]) * factor).astype(BF16)

        @pl.when(first & (m == 0))
        def _():
            pass_cache()
            stack_cache()

        item_mix()
        result = h1_buf[...] + dot(mix[...], witem[...])
        h_out[m] = result.astype(BF16)

        @pl.when(sends)
        def _():
            h_copy(m, section + 1).start()

        for pair in range(pairs):
            for at, place in enumerate(spread(pair)):
                wide[place, :] = result[at * rows_n : (at + 1) * rows_n, pair * pair_w : (pair + 1) * pair_w]
        staged[m] = wide[...].reshape(feats, block_n, pair_w).astype(BF16)
        out_copy(m, mine).start()
        out_own(m).start()
        return carry

    lax.fori_loop(0, micro, step, 0)

    for m in range(micro):
        out_own(m).wait()
        out_copy(m, theirs).wait()

    @pl.when(first)
    def _():
        for m in range(micro):
            x_copy(m, feat).wait_send()

    @pl.when(sends)
    def _():
        for m in range(micro):
            h_copy(m, section + 1).wait_send()

    for off in range(1, row_devs):
        cache_copy(off).wait_send()
    for off in range(row_devs):
        cache_pass(off, feat).wait_send()


def hand_over(source, target):
    target[...] = source[...]


def per_device(sizes, test_rows, train_cache, pattern, feat_qkv, feat_out, item_query, item_out, gains):
    sections, row_devs = sizes
    micro, test_n, gd, width = test_rows.shape
    train_dev = train_cache.shape[2]
    feats = 2
    rows_n = test_n // feats
    tokens = test_n * gd
    nk = row_devs * train_dev * gd
    pair_w = 2 * (width // HEADS)
    pairs = width // pair_w
    anywhere = pl.BlockSpec(memory_space=pl.ANY)
    vmem = pl.BlockSpec(memory_space=pltpu.VMEM)
    dma = pltpu.SemaphoreType.DMA
    per_row = gd * pairs

    def as_rows(x):
        pieces = x.reshape(x.shape[:-1] + (pairs, pair_w)).swapaxes(-3, -2)
        return pieces.reshape(x.shape[:-3] + (x.shape[-3] * per_row, pair_w))

    hidden = pl.pallas_call(
        functools.partial(kernel, sizes),
        out_shape=jax.ShapeDtypeStruct((1, micro, test_n * per_row, pair_w), BF16),
        in_specs=[anywhere, anywhere, vmem, anywhere, anywhere, anywhere, anywhere, vmem],
        out_specs=anywhere,
        scratch_shapes=[
            pltpu.VMEM((micro, feats, rows_n * per_row, pair_w), BF16),
            pltpu.VMEM((width, 3 * width), BF16),
            pltpu.VMEM((width, width), BF16),
            pltpu.VMEM((width, width), BF16),
            pltpu.VMEM((width, width), BF16),
            pltpu.VMEM((micro, tokens, width), BF16),
            pltpu.VMEM((micro, tokens, width), BF16),
            pltpu.VMEM((feats, row_devs, 2, train_dev * per_row, pair_w), BF16),
            pltpu.VMEM((feats, pairs, 2 * nk, pair_w), BF16),
            pltpu.VMEM((feats, pairs, 2 * nk, 2 * pair_w), BF16),
            pltpu.VMEM((2 * tokens, tokens), F32),
            pltpu.VMEM((tokens // feats, 2 * nk), F32),
            pltpu.VMEM((micro, feats, rows_n * per_row, pair_w), BF16),
            pltpu.VMEM((test_n * per_row, pair_w), F32),
            pltpu.VMEM((row_devs * train_dev * per_row, pair_w), F32),
            pltpu.VMEM((tokens, 3 * width), F32),
            pltpu.VMEM((tokens, width), BF16),
            pltpu.VMEM((tokens, width), BF16),
            pltpu.VMEM((tokens, width), F32),
            dma((4,)),
            dma((micro,)),
            dma(()),
            dma((micro,)),
            dma((micro,)),
            dma((micro,)),
            dma((row_devs - 1,)),
            dma((row_devs,)),
            dma((row_devs,)),
            dma((row_devs,)),
            dma((micro,)),
            dma((micro,)),
            dma((micro,)),
            dma((micro,)),
        ],
        compiler_params=pltpu.CompilerParams(
            collective_id=0, has_side_effects=True, vmem_limit_bytes=60 * 1024 * 1024
        ),
    )(as_rows(test_rows), as_rows(train_cache), pattern, feat_qkv, feat_out, item_query, item_out, gains)
    hidden = pl.pallas_call(
        hand_over,
        out_shape=jax.ShapeDtypeStruct(hidden.shape, hidden.dtype),
        in_specs=[vmem],
        out_specs=vmem,
        compiler_params=pltpu.CompilerParams(vmem_limit_bytes=60 * 1024 * 1024),
    )(hidden)
    hidden = hidden.reshape(1, micro, test_n, pairs, gd, pair_w).swapaxes(-3, -2)
    return hidden.reshape(1, micro, test_n, gd, width)


def solution(mesh):
    sizes = (mesh.shape["section"], mesh.shape["rows"])
    return jax.shard_map(
        functools.partial(per_device, sizes),
        mesh=mesh,
        in_specs=(
            P(None, ("groups", "rows"), "feat", None),
            P("section", None, ("groups", "rows"), "feat", None),
            P(),
            P("section", None, None),
            P("section", None, None),
            P("section", None, None),
            P("section", None, None),
            P("section", None, None),
        ),
        out_specs=P("section", None, ("groups", "rows"), "feat", None),
        check_vma=False,
    )
```

```python
import functools
import math

import jax
import jax.numpy as jnp
from jax import lax
from jax.experimental import pallas as pl
from jax.experimental.pallas import tpu as pltpu
from jax.sharding import PartitionSpec as P

HEADS = 8
MESH = pl.DeviceIdType.MESH
F32 = jnp.float32
BF16 = jnp.bfloat16
EXCLUDED = -1e30
SUB = 8
VMEM_GRANT = 60 * 1024 * 1024


def iota(shape, dim):
    return lax.broadcasted_iota(jnp.int32, shape, dim)


def normed(x, gain):
    mean_sq = jnp.mean(x * x, axis=-1, keepdims=True)
    return (x * lax.rsqrt(mean_sq + 1e-06) * gain).astype(BF16)


def dot(a, b):
    return jnp.dot(a, b, preferred_element_type=F32)


def dot_t(a, b):
    return lax.dot_general(a, b, (((1,), (1,)), ((), ())), preferred_element_type=F32)


def kernel(
    sizes, rows_hbm, cache_hbm, pattern_ref, qkv_hbm, out_hbm, query_hbm, item_hbm, gains_ref, hidden_hbm,
    x_buf, wqkv, wout, wquery, witem, h_buf, h_out, cache_buf, k_stack, v_stack, feat_bias, item_bias, staged, wide, cache_wide,
    weight_sem, x_sem, own_sem, out_sem, x_send, x_recv, cache_send, cache_recv, pass_send, pass_recv,
    h_send, h_recv, out_send, out_recv,
):
    sections, row_devs = sizes
    micro, tokens, width = h_buf.shape
    feats = x_buf.shape[1]
    pair_w = 2 * (width // HEADS)
    pairs = width // pair_w
    half = tokens // feats
    gd = pattern_ref.shape[0] // feats
    rows_n = half // gd
    per_row = gd * pairs
    train_n = cache_wide.shape[0] // per_row
    nk = train_n * gd
    blocks = rows_n // SUB
    block_t = tokens // blocks
    span_t = gd * SUB
    factor = math.log2(math.e) / math.sqrt(width // HEADS)

    section = lax.axis_index("section")
    row = lax.axis_index("rows")
    feat = lax.axis_index("feat")
    partner = 1 - feat
    first = section == 0
    receives = section > 0
    sends = section < sections - 1
    block_n = rows_n * per_row
    mine = pl.ds(feat * block_n, block_n)
    theirs = pl.ds(partner * block_n, block_n)

    weights = [
        pltpu.make_async_copy(src.at[0], dst, weight_sem.at[i])
        for i, (src, dst) in enumerate(
            [(qkv_hbm, wqkv), (out_hbm, wout), (query_hbm, wquery), (item_hbm, witem)]
        )
    ]

    def x_own(m):
        return pltpu.make_async_copy(rows_hbm.at[m, mine], x_buf.at[m, feat], x_sem.at[m])

    @pl.when(first)
    def _():
        for m in range(micro):
            x_own(m).start()

    weights[0].start()
    own_cache = pltpu.make_async_copy(cache_hbm.at[0], cache_buf.at[feat, row], own_sem)
    own_cache.start()

    barrier = pltpu.get_barrier_semaphore()
    pl.semaphore_signal(barrier, inc=1, device_id={"feat": partner}, device_id_type=MESH)
    for off in range(1, row_devs):
        pl.semaphore_signal(
            barrier, inc=1, device_id={"rows": lax.rem(row + off, row_devs)}, device_id_type=MESH
        )

    @pl.when(receives)
    def _():
        pl.semaphore_signal(barrier, inc=1, device_id={"section": section - 1}, device_id_type=MESH)

    @pl.when(sends)
    def _():
        pl.semaphore_signal(barrier, inc=1, device_id={"section": section + 1}, device_id_type=MESH)

    pl.semaphore_wait(
        barrier, row_devs + jnp.where(receives, 1, 0) + jnp.where(sends, 1, 0)
    )

    def x_copy(m, source):
        return pltpu.make_async_remote_copy(
            src_ref=rows_hbm.at[m, theirs], dst_ref=x_buf.at[m, source],
            send_sem=x_send.at[m], recv_sem=x_recv.at[m],
            device_id={"feat": partner}, device_id_type=MESH,
        )

    def cache_copy(off):
        return pltpu.make_async_remote_copy(
            src_ref=cache_hbm.at[0], dst_ref=cache_buf.at[feat, row],
            send_sem=cache_send.at[off - 1], recv_sem=cache_recv.at[row],
            device_id={"rows": lax.rem(row + off, row_devs)}, device_id_type=MESH,
        )

    def cache_arrival(off):
        source = lax.rem(row + off, row_devs)
        return pltpu.make_async_remote_copy(
            src_ref=cache_hbm.at[0], dst_ref=cache_buf.at[feat, source],
            send_sem=cache_send.at[off - 1], recv_sem=cache_recv.at[source],
            device_id={"rows": source}, device_id_type=MESH,
        )

    def cache_pass(off, source_feat):
        source = lax.rem(row + off, row_devs)
        return pltpu.make_async_remote_copy(
            src_ref=cache_hbm.at[0] if off == 0 else cache_buf.at[feat, source],
            dst_ref=cache_buf.at[source_feat, source],
            send_sem=pass_send.at[off], recv_sem=pass_recv.at[off],
            device_id={"feat": partner}, device_id_type=MESH,
        )

    @pl.when(first)
    def _():
        x_copy(0, feat).start()

    for off in range(1, row_devs):
        cache_copy(off).start()

    @pl.when(first)
    def _():
        for m in range(1, micro):
            x_copy(m, feat).start()

    cache_pass(0, feat).start()
    for copy in weights[1:]:
        copy.start()

    def h_copy(m, target):
        return pltpu.make_async_remote_copy(
            src_ref=h_out.at[m], dst_ref=h_buf.at[m],
            send_sem=h_send.at[m], recv_sem=h_recv.at[m],
            device_id={"section": target}, device_id_type=MESH,
        )

    def out_own(m):
        return pltpu.make_async_copy(staged.at[m, feat], hidden_hbm.at[0, m, mine], out_sem.at[m])

    def out_copy(m, place):
        return pltpu.make_async_remote_copy(
            src_ref=staged.at[m, partner], dst_ref=hidden_hbm.at[0, m, place],
            send_sem=out_send.at[m], recv_sem=out_recv.at[m],
            device_id={"feat": partner}, device_id_type=MESH,
        )

    groups = feats * gd
    nf = block_t
    pick_q = (iota((nf, groups), 0) // SUB == iota((nf, groups), 1)).astype(F32)
    pick_k = ((iota((groups, 2 * nf), 1) % nf) // SUB == iota((groups, 2 * nf), 0)).astype(F32)
    pattern = (pattern_ref[...] != 0).astype(F32)
    seen = dot(dot(pick_q, pattern), pick_k) > 0.5
    qi, ki = iota((nf, 2 * nf), 0), iota((nf, 2 * nf), 1) % nf
    seen = (seen | (qi == ki)) & (qi % SUB == ki % SUB)
    feat_bias[...] = jnp.where(seen, 0.0, EXCLUDED).astype(F32)
    item_bias[...] = jnp.where(
        (iota((half, 2 * nk), 0) % span_t) // SUB == (iota((half, 2 * nk), 1) % nk) // train_n, 0.0, EXCLUDED
    ).astype(F32)

    def pass_cache():
        for off in range(1, row_devs):
            cache_arrival(off).wait_recv()
            cache_pass(off, feat).start()

    def stack_cache():
        own_cache.wait()
        for off in range(row_devs):
            cache_pass(off, partner).wait_recv()
        side = iota((nk, pair_w), 1) < pair_w // 2
        one = jnp.where(side, 1.0, 0.0).astype(BF16)
        other = jnp.where(side, 0.0, 1.0).astype(BF16)
        for f in range(feats):
            for kind in range(2):
                cache_wide[...] = cache_buf[f, :, kind].astype(F32).reshape(cache_wide.shape)
                for pair in range(pairs):
                    part = jnp.concatenate(
                        [cache_wide[pl.ds(pair * gd + g, train_n, stride=per_row), :] for g in range(gd)], axis=0
                    )
                    low = jnp.where(side, part, 0.0).astype(BF16)
                    high = jnp.where(side, 0.0, part).astype(BF16)
                    if kind == 0:
                        k_stack[f, pair, :nk] = low
                        k_stack[f, pair, nk:] = high
                    else:
                        v_stack[f, pair, :nk, :pair_w] = low
                        v_stack[f, pair, nk:, :pair_w] = high
                        v_stack[f, pair, :nk, pair_w:] = one
                        v_stack[f, pair, nk:, pair_w:] = other

    low_half = iota((tokens, pair_w), 1) < pair_w // 2
    low_ones = jnp.where(low_half[:nf], 1.0, 0.0).astype(BF16)
    high_ones = jnp.where(low_half[:nf], 0.0, 1.0).astype(BF16)
    ones = jnp.concatenate([low_ones, high_ones], axis=0)

    def attend(s, values, n):
        first_keys = iota(s.shape, 1) < n
        low = jnp.max(jnp.where(first_keys, s, -jnp.inf), axis=-1, keepdims=True)
        high = jnp.max(jnp.where(first_keys, -jnp.inf, s), axis=-1, keepdims=True)
        p = jnp.exp2(s - jnp.where(first_keys, low, high)).astype(BF16)
        o = dot(p, values)
        return (o[:, :pair_w] * pl.reciprocal(o[:, pair_w:], approx=True)).astype(BF16)

    def feature_mix(q, k, v):
        mixed = []
        for pair in range(pairs):
            lanes = slice(pair * pair_w, (pair + 1) * pair_w)
            k_low = jnp.where(low_half, k[:, lanes], 0.0).astype(BF16)
            k_high = jnp.where(low_half, 0.0, k[:, lanes]).astype(BF16)
            v_low = jnp.where(low_half, v[:, lanes], 0.0).astype(BF16)
            v_high = jnp.where(low_half, 0.0, v[:, lanes]).astype(BF16)
            parts = []
            for block in range(blocks):
                at = slice(block * nf, (block + 1) * nf)
                keys = jnp.concatenate([k_low[at], k_high[at]], axis=0)
                values = jnp.concatenate([v_low[at], v_high[at]], axis=0)
                s = dot_t(q[at, lanes], keys) + feat_bias[...]
                parts.append(attend(s, jnp.concatenate([values, ones], axis=1), nf))
            mixed.append(jnp.concatenate(parts, axis=0))
        return jnp.concatenate(mixed, axis=1)

    def item_mix(query):
        pieces = [[None] * feats for _ in range(blocks)]
        for f in range(feats):
            at = [slice((b * feats + f) * span_t, (b * feats + f + 1) * span_t) for b in range(blocks)]
            mixed = []
            for pair in range(pairs):
                lanes = slice(pair * pair_w, (pair + 1) * pair_w)
                q = jnp.concatenate([query[span, lanes] for span in at], axis=0)
                mixed.append(attend(dot_t(q, k_stack[f, pair]) + item_bias[...], v_stack[f, pair], nk))
            mixed = jnp.concatenate(mixed, axis=1)
            for b in range(blocks):
                pieces[b][f] = mixed[b * span_t : (b + 1) * span_t]
        return jnp.concatenate([piece for row_pieces in pieces for piece in row_pieces], axis=0)

    @pl.when(receives)
    def _():
        pass_cache()
        stack_cache()

    weights[0].wait()

    def spread(pair):
        return [
            pl.ds(f * block_n + b * SUB * per_row + pair * gd + g, SUB, stride=per_row)
            for b in range(blocks)
            for f in range(feats)
            for g in range(gd)
        ]

    def step(m, carry):
        @pl.when(first)
        def _():
            x_own(m).wait()
            x_copy(m, partner).wait_recv()
            wide[...] = x_buf[m].astype(F32).reshape(wide.shape)
            for pair in range(pairs):
                part = [wide[place, :] for place in spread(pair)]
                lanes = slice(pair * pair_w, (pair + 1) * pair_w)
                h_buf[m, :, lanes] = jnp.concatenate(part, axis=0).astype(BF16)

        @pl.when(receives)
        def _():
            h_copy(m, section - 1).wait_recv()

        h = h_buf[m].astype(F32)
        a = normed(h, gains_ref[0, 0:1, :])
        q = (dot(a, wqkv[:, :width]) * factor).astype(BF16)
        k = dot(a, wqkv[:, width : 2 * width])
        v = dot(a, wqkv[:, 2 * width :])

        @pl.when(m == 0)
        def _():
            for copy in weights[1:]:
                copy.wait()

        h1 = h + dot(feature_mix(q, k, v), wout[...])
        b = normed(h1, gains_ref[0, 1:2, :])
        query = (dot(b, wquery[...]) * factor).astype(BF16)

        @pl.when(first & (m == 0))
        def _():
            pass_cache()
            stack_cache()

        result = h1 + dot(item_mix(query), witem[...])
        h_out[m] = result.astype(BF16)

        @pl.when(sends)
        def _():
            h_copy(m, section + 1).start()

        for pair in range(pairs):
            for at, place in enumerate(spread(pair)):
                wide[place, :] = result[at * SUB : (at + 1) * SUB, pair * pair_w : (pair + 1) * pair_w]
        staged[m] = wide[...].reshape(feats, block_n, pair_w).astype(BF16)
        out_copy(m, mine).start()
        out_own(m).start()
        return carry

    lax.fori_loop(0, micro, step, 0)

    for m in range(micro):
        out_own(m).wait()
        out_copy(m, theirs).wait()

    @pl.when(first)
    def _():
        for m in range(micro):
            x_copy(m, feat).wait_send()

    @pl.when(sends)
    def _():
        for m in range(micro):
            h_copy(m, section + 1).wait_send()

    for off in range(1, row_devs):
        cache_copy(off).wait_send()
    for off in range(row_devs):
        cache_pass(off, feat).wait_send()


def per_device(sizes, test_rows, train_cache, pattern, feat_qkv, feat_out, item_query, item_out, gains):
    sections, row_devs = sizes
    micro, test_n, gd, width = test_rows.shape
    train_dev = train_cache.shape[2]
    feats = 2
    rows_n = test_n // feats
    tokens = test_n * gd
    nk = row_devs * train_dev * gd
    pair_w = 2 * (width // HEADS)
    pairs = width // pair_w
    anywhere = pl.BlockSpec(memory_space=pl.ANY)
    vmem = pl.BlockSpec(memory_space=pltpu.VMEM)
    dma = pltpu.SemaphoreType.DMA
    per_row = gd * pairs

    def as_rows(x):
        pieces = x.reshape(x.shape[:-1] + (pairs, pair_w)).swapaxes(-3, -2)
        return pieces.reshape(x.shape[:-3] + (x.shape[-3] * per_row, pair_w))

    hidden = pl.pallas_call(
        functools.partial(kernel, sizes),
        out_shape=jax.ShapeDtypeStruct((1, micro, test_n * per_row, pair_w), BF16),
        in_specs=[anywhere, anywhere, vmem, anywhere, anywhere, anywhere, anywhere, vmem],
        out_specs=anywhere,
        scratch_shapes=[
            pltpu.VMEM((micro, feats, rows_n * per_row, pair_w), BF16),
            pltpu.VMEM((width, 3 * width), BF16),
            pltpu.VMEM((width, width), BF16),
            pltpu.VMEM((width, width), BF16),
            pltpu.VMEM((width, width), BF16),
            pltpu.VMEM((micro, tokens, width), BF16),
            pltpu.VMEM((micro, tokens, width), BF16),
            pltpu.VMEM((feats, row_devs, 2, train_dev * per_row, pair_w), BF16),
            pltpu.VMEM((feats, pairs, 2 * nk, pair_w), BF16),
            pltpu.VMEM((feats, pairs, 2 * nk, 2 * pair_w), BF16),
            pltpu.VMEM((SUB * gd * feats, 2 * SUB * gd * feats), F32),
            pltpu.VMEM((tokens // feats, 2 * nk), F32),
            pltpu.VMEM((micro, feats, rows_n * per_row, pair_w), BF16),
            pltpu.VMEM((test_n * per_row, pair_w), F32),
            pltpu.VMEM((row_devs * train_dev * per_row, pair_w), F32),
            dma((4,)),
            dma((micro,)),
            dma(()),
            dma((micro,)),
            dma((micro,)),
            dma((micro,)),
            dma((row_devs - 1,)),
            dma((row_devs,)),
            dma((row_devs,)),
            dma((row_devs,)),
            dma((micro,)),
            dma((micro,)),
            dma((micro,)),
            dma((micro,)),
        ],
        compiler_params=pltpu.CompilerParams(
            collective_id=0, has_side_effects=True, vmem_limit_bytes=VMEM_GRANT
        ),
    )(as_rows(test_rows), as_rows(train_cache), pattern, feat_qkv, feat_out, item_query, item_out, gains)
    hidden = hidden.reshape(1, micro, test_n, pairs, gd, pair_w).swapaxes(-3, -2)
    return hidden.reshape(1, micro, test_n, gd, width)


def solution(mesh):
    sizes = (mesh.shape["section"], mesh.shape["rows"])
    return jax.shard_map(
        functools.partial(per_device, sizes),
        mesh=mesh,
        in_specs=(
            P(None, ("groups", "rows"), "feat", None),
            P("section", None, ("groups", "rows"), "feat", None),
            P(),
            P("section", None, None),
            P("section", None, None),
            P("section", None, None),
            P("section", None, None),
            P("section", None, None),
        ),
        out_specs=P("section", None, ("groups", "rows"), "feat", None),
        check_vma=False,
    )
```

```python
import functools
import math

import jax
import jax.numpy as jnp
from jax import lax
from jax.experimental import pallas as pl
from jax.experimental.pallas import tpu as pltpu
from jax.sharding import PartitionSpec as P

HEADS = 8
MESH = pl.DeviceIdType.MESH
F32 = jnp.float32
BF16 = jnp.bfloat16
EXCLUDED = -1e30
VMEM_GRANT = 60 * 1024 * 1024


def iota(shape, dim):
    return lax.broadcasted_iota(jnp.int32, shape, dim)


def normed(x, gain):
    mean_sq = jnp.mean(x * x, axis=-1, keepdims=True)
    return (x * lax.rsqrt(mean_sq + 1e-06) * gain).astype(BF16)


def dot(a, b):
    return jnp.dot(a, b, preferred_element_type=F32)


def dot_t(a, b):
    return lax.dot_general(a, b, (((1,), (1,)), ((), ())), preferred_element_type=F32)


def kernel(
    sizes, rows_hbm, cache_hbm, pattern_ref, qkv_hbm, out_hbm, query_hbm, item_hbm, gains_ref, hidden_hbm,
    x_buf, wqkv, wout, wquery, witem, h_buf, h_out, cache_buf, k_stack, v_stack, feat_bias, item_bias, staged, wide, cache_wide,
    weight_sem, x_sem, own_sem, out_sem, x_send, x_recv, cache_send, cache_recv, pass_send, pass_recv,
    h_send, h_recv, out_send, out_recv,
):
    sections, row_devs = sizes
    micro, tokens, width = h_buf.shape
    feats = x_buf.shape[1]
    pair_w = 2 * (width // HEADS)
    pairs = width // pair_w
    half = tokens // feats
    gd = pattern_ref.shape[0] // feats
    rows_n = half // gd
    per_row = gd * pairs
    train_n = cache_wide.shape[0] // per_row
    nk = train_n * gd
    factor = math.log2(math.e) / math.sqrt(width // HEADS)

    section = lax.axis_index("section")
    row = lax.axis_index("rows")
    feat = lax.axis_index("feat")
    partner = 1 - feat
    first = section == 0
    receives = section > 0
    sends = section < sections - 1
    block_n = rows_n * per_row
    mine = pl.ds(feat * block_n, block_n)
    theirs = pl.ds(partner * block_n, block_n)

    weights = [
        pltpu.make_async_copy(src.at[0], dst, weight_sem.at[i])
        for i, (src, dst) in enumerate(
            [(qkv_hbm, wqkv), (out_hbm, wout), (query_hbm, wquery), (item_hbm, witem)]
        )
    ]

    def x_own(m):
        return pltpu.make_async_copy(rows_hbm.at[m, mine], x_buf.at[m, feat], x_sem.at[m])

    @pl.when(first)
    def _():
        for m in range(micro):
            x_own(m).start()

    weights[0].start()
    own_cache = pltpu.make_async_copy(cache_hbm.at[0], cache_buf.at[feat, row], own_sem)
    own_cache.start()

    barrier = pltpu.get_barrier_semaphore()
    pl.semaphore_signal(barrier, inc=1, device_id={"feat": partner}, device_id_type=MESH)
    for off in range(1, row_devs):
        pl.semaphore_signal(
            barrier, inc=1, device_id={"rows": lax.rem(row + off, row_devs)}, device_id_type=MESH
        )

    @pl.when(receives)
    def _():
        pl.semaphore_signal(barrier, inc=1, device_id={"section": section - 1}, device_id_type=MESH)

    @pl.when(sends)
    def _():
        pl.semaphore_signal(barrier, inc=1, device_id={"section": section + 1}, device_id_type=MESH)

    pl.semaphore_wait(
        barrier, row_devs + jnp.where(receives, 1, 0) + jnp.where(sends, 1, 0)
    )

    def x_copy(m, source):
        return pltpu.make_async_remote_copy(
            src_ref=rows_hbm.at[m, theirs], dst_ref=x_buf.at[m, source],
            send_sem=x_send.at[m], recv_sem=x_recv.at[m],
            device_id={"feat": partner}, device_id_type=MESH,
        )

    def cache_copy(off):
        return pltpu.make_async_remote_copy(
            src_ref=cache_hbm.at[0], dst_ref=cache_buf.at[feat, row],
            send_sem=cache_send.at[off - 1], recv_sem=cache_recv.at[row],
            device_id={"rows": lax.rem(row + off, row_devs)}, device_id_type=MESH,
        )

    def cache_arrival(off):
        source = lax.rem(row + off, row_devs)
        return pltpu.make_async_remote_copy(
            src_ref=cache_hbm.at[0], dst_ref=cache_buf.at[feat, source],
            send_sem=cache_send.at[off - 1], recv_sem=cache_recv.at[source],
            device_id={"rows": source}, device_id_type=MESH,
        )

    def cache_pass(off, source_feat):
        source = lax.rem(row + off, row_devs)
        return pltpu.make_async_remote_copy(
            src_ref=cache_hbm.at[0] if off == 0 else cache_buf.at[feat, source],
            dst_ref=cache_buf.at[source_feat, source],
            send_sem=pass_send.at[off], recv_sem=pass_recv.at[off],
            device_id={"feat": partner}, device_id_type=MESH,
        )

    @pl.when(first)
    def _():
        x_copy(0, feat).start()

    for off in range(1, row_devs):
        cache_copy(off).start()

    @pl.when(first)
    def _():
        for m in range(1, micro):
            x_copy(m, feat).start()

    cache_pass(0, feat).start()
    for copy in weights[1:]:
        copy.start()

    def h_copy(m, target):
        return pltpu.make_async_remote_copy(
            src_ref=h_out.at[m], dst_ref=h_buf.at[m],
            send_sem=h_send.at[m], recv_sem=h_recv.at[m],
            device_id={"section": target}, device_id_type=MESH,
        )

    def out_own(m):
        return pltpu.make_async_copy(staged.at[m, feat], hidden_hbm.at[0, m, mine], out_sem.at[m])

    def out_copy(m, place):
        return pltpu.make_async_remote_copy(
            src_ref=staged.at[m, partner], dst_ref=hidden_hbm.at[0, m, place],
            send_sem=out_send.at[m], recv_sem=out_recv.at[m],
            device_id={"feat": partner}, device_id_type=MESH,
        )

    groups = feats * gd
    pick_q = (iota((tokens, groups), 0) // rows_n == iota((tokens, groups), 1)).astype(F32)
    pick_k = (iota((groups, tokens), 1) // rows_n == iota((groups, tokens), 0)).astype(F32)
    pattern = (pattern_ref[...] != 0).astype(F32)
    seen = dot(dot(pick_q, pattern), pick_k) > 0.5
    qi, ki = iota((tokens, tokens), 0), iota((tokens, tokens), 1)
    seen = (seen | (qi == ki)) & (qi % rows_n == ki % rows_n)
    bias = jnp.where(seen, 0.0, EXCLUDED).astype(F32)
    feat_bias[:tokens] = bias
    feat_bias[tokens:] = bias
    item_bias[...] = jnp.where(
        iota((half, 2 * nk), 0) // rows_n == (iota((half, 2 * nk), 1) % nk) // train_n, 0.0, EXCLUDED
    ).astype(F32)

    def pass_cache():
        for off in range(1, row_devs):
            cache_arrival(off).wait_recv()
            cache_pass(off, feat).start()

    def stack_cache():
        own_cache.wait()
        for off in range(row_devs):
            cache_pass(off, partner).wait_recv()
        side = iota((nk, pair_w), 1) < pair_w // 2
        one = jnp.where(side, 1.0, 0.0).astype(BF16)
        other = jnp.where(side, 0.0, 1.0).astype(BF16)
        for f in range(feats):
            for kind in range(2):
                cache_wide[...] = cache_buf[f, :, kind].astype(F32).reshape(cache_wide.shape)
                for pair in range(pairs):
                    part = jnp.concatenate(
                        [cache_wide[pl.ds(pair * gd + g, train_n, stride=per_row), :] for g in range(gd)], axis=0
                    )
                    low = jnp.where(side, part, 0.0).astype(BF16)
                    high = jnp.where(side, 0.0, part).astype(BF16)
                    if kind == 0:
                        k_stack[f, pair, :nk] = low
                        k_stack[f, pair, nk:] = high
                    else:
                        v_stack[f, pair, :nk, :pair_w] = low
                        v_stack[f, pair, nk:, :pair_w] = high
                        v_stack[f, pair, :nk, pair_w:] = one
                        v_stack[f, pair, nk:, pair_w:] = other

    low_half = iota((tokens, pair_w), 1) < pair_w // 2
    low_lanes = iota((tokens, width), 1) % pair_w < pair_w // 2
    ones = jnp.ones((tokens, pair_w), BF16)

    tiles = [slice(pair * pair_w, (pair + 1) * pair_w) for pair in range(pairs)]

    def feature_mix(q, k, v):
        low = jnp.where(low_lanes, q, 0.0).astype(BF16)
        high = jnp.where(low_lanes, 0.0, q).astype(BF16)
        queries = [jnp.concatenate([low[:, lanes], high[:, lanes]], axis=0) for lanes in tiles]
        scores = [dot_t(q2, k[:, lanes]) for q2, lanes in zip(queries, tiles)]
        scores = [s + feat_bias[...] for s in scores]
        tops = [jnp.max(s, axis=-1, keepdims=True) for s in scores]
        weights_of = [jnp.exp2(s - top).astype(BF16) for s, top in zip(scores, tops)]
        sums = [
            dot(p, jnp.concatenate([v[:, lanes], ones], axis=1)) for p, lanes in zip(weights_of, tiles)
        ]
        mixed = []
        for o in sums:
            total = jnp.where(low_half, o[:tokens, pair_w:], o[tokens:, pair_w:])
            o = jnp.where(low_half, o[:tokens, :pair_w], o[tokens:, :pair_w])
            mixed.append((o * pl.reciprocal(total, approx=True)).astype(BF16))
        return jnp.concatenate(mixed, axis=1)

    low_keys = iota((half, 2 * nk), 1) < nk

    def item_mix(query):
        units = [(f, pair) for f in range(feats) for pair in range(pairs)]
        scores = [
            dot_t(query[f * half : (f + 1) * half, tiles[pair]], k_stack[f, pair]) for f, pair in units
        ]
        scores = [s + item_bias[...] for s in scores]
        lows = [jnp.max(jnp.where(low_keys, s, -jnp.inf), axis=-1, keepdims=True) for s in scores]
        highs = [jnp.max(jnp.where(low_keys, -jnp.inf, s), axis=-1, keepdims=True) for s in scores]
        weights_of = [
            jnp.exp2(s - jnp.where(low_keys, low, high)).astype(BF16)
            for s, low, high in zip(scores, lows, highs)
        ]
        sums = [dot(p, v_stack[f, pair]) for p, (f, pair) in zip(weights_of, units)]
        mixed = [(o[:, :pair_w] * pl.reciprocal(o[:, pair_w:], approx=True)).astype(BF16) for o in sums]
        blocks = [jnp.concatenate(mixed[f * pairs : (f + 1) * pairs], axis=1) for f in range(feats)]
        return jnp.concatenate(blocks, axis=0)

    @pl.when(receives)
    def _():
        pass_cache()
        stack_cache()

    weights[0].wait()

    def spread(pair):
        return [
            pl.ds(f * block_n + pair * gd + g, rows_n, stride=per_row)
            for f in range(feats)
            for g in range(gd)
        ]

    def step(m, carry):
        @pl.when(first)
        def _():
            x_own(m).wait()
            x_copy(m, partner).wait_recv()
            wide[...] = x_buf[m].astype(F32).reshape(wide.shape)
            for pair in range(pairs):
                part = [wide[place, :] for place in spread(pair)]
                lanes = slice(pair * pair_w, (pair + 1) * pair_w)
                h_buf[m, :, lanes] = jnp.concatenate(part, axis=0).astype(BF16)

        @pl.when(receives)
        def _():
            h_copy(m, section - 1).wait_recv()

        h = h_buf[m].astype(F32)
        a = normed(h, gains_ref[0, 0:1, :])
        q = dot(a, wqkv[:, :width]) * factor
        k = dot(a, wqkv[:, width : 2 * width]).astype(BF16)
        v = dot(a, wqkv[:, 2 * width :]).astype(BF16)

        @pl.when(m == 0)
        def _():
            for copy in weights[1:]:
                copy.wait()

        h1 = h + dot(feature_mix(q, k, v), wout[...])
        b = normed(h1, gains_ref[0, 1:2, :])
        query = (dot(b, wquery[...]) * factor).astype(BF16)

        @pl.when(first & (m == 0))
        def _():
            pass_cache()
            stack_cache()

        result = h1 + dot(item_mix(query), witem[...])
        h_out[m] = result.astype(BF16)

        @pl.when(sends)
        def _():
            h_copy(m, section + 1).start()

        for pair in range(pairs):
            for at, place in enumerate(spread(pair)):
                wide[place, :] = result[at * rows_n : (at + 1) * rows_n, pair * pair_w : (pair + 1) * pair_w]
        staged[m] = wide[...].reshape(feats, block_n, pair_w).astype(BF16)
        out_copy(m, mine).start()
        out_own(m).start()
        return carry

    lax.fori_loop(0, micro, step, 0)

    for m in range(micro):
        out_own(m).wait()
        out_copy(m, theirs).wait()

    @pl.when(first)
    def _():
        for m in range(micro):
            x_copy(m, feat).wait_send()

    @pl.when(sends)
    def _():
        for m in range(micro):
            h_copy(m, section + 1).wait_send()

    for off in range(1, row_devs):
        cache_copy(off).wait_send()
    for off in range(row_devs):
        cache_pass(off, feat).wait_send()


def per_device(sizes, test_rows, train_cache, pattern, feat_qkv, feat_out, item_query, item_out, gains):
    sections, row_devs = sizes
    micro, test_n, gd, width = test_rows.shape
    train_dev = train_cache.shape[2]
    feats = 2
    rows_n = test_n // feats
    tokens = test_n * gd
    nk = row_devs * train_dev * gd
    pair_w = 2 * (width // HEADS)
    pairs = width // pair_w
    anywhere = pl.BlockSpec(memory_space=pl.ANY)
    vmem = pl.BlockSpec(memory_space=pltpu.VMEM)
    dma = pltpu.SemaphoreType.DMA
    per_row = gd * pairs

    def as_rows(x):
        pieces = x.reshape(x.shape[:-1] + (pairs, pair_w)).swapaxes(-3, -2)
        return pieces.reshape(x.shape[:-3] + (x.shape[-3] * per_row, pair_w))

    hidden = pl.pallas_call(
        functools.partial(kernel, sizes),
        out_shape=jax.ShapeDtypeStruct((1, micro, test_n * per_row, pair_w), BF16),
        in_specs=[anywhere, anywhere, vmem, anywhere, anywhere, anywhere, anywhere, vmem],
        out_specs=anywhere,
        scratch_shapes=[
            pltpu.VMEM((micro, feats, rows_n * per_row, pair_w), BF16),
            pltpu.VMEM((width, 3 * width), BF16),
            pltpu.VMEM((width, width), BF16),
            pltpu.VMEM((width, width), BF16),
            pltpu.VMEM((width, width), BF16),
            pltpu.VMEM((micro, tokens, width), BF16),
            pltpu.VMEM((micro, tokens, width), BF16),
            pltpu.VMEM((feats, row_devs, 2, train_dev * per_row, pair_w), BF16),
            pltpu.VMEM((feats, pairs, 2 * nk, pair_w), BF16),
            pltpu.VMEM((feats, pairs, 2 * nk, 2 * pair_w), BF16),
            pltpu.VMEM((2 * tokens, tokens), F32),
            pltpu.VMEM((tokens // feats, 2 * nk), F32),
            pltpu.VMEM((micro, feats, rows_n * per_row, pair_w), BF16),
            pltpu.VMEM((test_n * per_row, pair_w), F32),
            pltpu.VMEM((row_devs * train_dev * per_row, pair_w), F32),
            dma((4,)),
            dma((micro,)),
            dma(()),
            dma((micro,)),
            dma((micro,)),
            dma((micro,)),
            dma((row_devs - 1,)),
            dma((row_devs,)),
            dma((row_devs,)),
            dma((row_devs,)),
            dma((micro,)),
            dma((micro,)),
            dma((micro,)),
            dma((micro,)),
        ],
        compiler_params=pltpu.CompilerParams(
            collective_id=0, has_side_effects=True, vmem_limit_bytes=VMEM_GRANT
        ),
    )(as_rows(test_rows), as_rows(train_cache), pattern, feat_qkv, feat_out, item_query, item_out, gains)
    hidden = hidden.reshape(1, micro, test_n, pairs, gd, pair_w).swapaxes(-3, -2)
    return hidden.reshape(1, micro, test_n, gd, width)


def solution(mesh):
    sizes = (mesh.shape["section"], mesh.shape["rows"])
    return jax.shard_map(
        functools.partial(per_device, sizes),
        mesh=mesh,
        in_specs=(
            P(None, ("groups", "rows"), "feat", None),
            P("section", None, ("groups", "rows"), "feat", None),
            P(),
            P("section", None, None),
            P("section", None, None),
            P("section", None, None),
            P("section", None, None),
            P("section", None, None),
        ),
        out_specs=P("section", None, ("groups", "rows"), "feat", None),
        check_vma=False,
    )
```

```python
import functools
import math

import jax
import jax.numpy as jnp
from jax import lax
from jax.experimental import pallas as pl
from jax.experimental.pallas import tpu as pltpu
from jax.sharding import PartitionSpec as P

HEADS = 8
MESH = pl.DeviceIdType.MESH
F32 = jnp.float32
BF16 = jnp.bfloat16
EXCLUDED = -1e30
VMEM_GRANT = 60 * 1024 * 1024


def iota(shape, dim):
    return lax.broadcasted_iota(jnp.int32, shape, dim)


def normed(x, gain):
    mean_sq = jnp.mean(x * x, axis=-1, keepdims=True)
    return (x * lax.rsqrt(mean_sq + 1e-06) * gain).astype(BF16)


def dot(a, b):
    return jnp.dot(a, b, preferred_element_type=F32)


def dot_t(a, b):
    return lax.dot_general(a, b, (((1,), (1,)), ((), ())), preferred_element_type=F32)


def kernel(
    sizes, rows_hbm, cache_hbm, pattern_ref, qkv_hbm, out_hbm, query_hbm, item_hbm, gains_ref, hidden_hbm,
    x_buf, wqkv, wout, wquery, witem, h_buf, h_out, cache_buf, k_stack, v_stack, feat_bias, item_bias, staged, wide, cache_wide,
    weight_sem, x_sem, own_sem, out_sem, x_send, x_recv, cache_send, cache_recv, pass_send, pass_recv,
    h_send, h_recv, out_send, out_recv,
):
    sections, row_devs = sizes
    micro, tokens, width = h_buf.shape
    feats = x_buf.shape[1]
    pair_w = 2 * (width // HEADS)
    pairs = width // pair_w
    half = tokens // feats
    gd = pattern_ref.shape[0] // feats
    rows_n = half // gd
    per_row = gd * pairs
    train_n = cache_wide.shape[0] // per_row
    nk = train_n * gd
    factor = math.log2(math.e) / math.sqrt(width // HEADS)

    section = lax.axis_index("section")
    row = lax.axis_index("rows")
    feat = lax.axis_index("feat")
    partner = 1 - feat
    first = section == 0
    receives = section > 0
    sends = section < sections - 1
    block_n = rows_n * per_row
    mine = pl.ds(feat * block_n, block_n)
    theirs = pl.ds(partner * block_n, block_n)

    weights = [
        pltpu.make_async_copy(src.at[0], dst, weight_sem.at[i])
        for i, (src, dst) in enumerate(
            [(qkv_hbm, wqkv), (out_hbm, wout), (query_hbm, wquery), (item_hbm, witem)]
        )
    ]

    def x_own(m):
        return pltpu.make_async_copy(rows_hbm.at[m, mine], x_buf.at[m, feat], x_sem.at[m])

    @pl.when(first)
    def _():
        for m in range(micro):
            x_own(m).start()

    weights[0].start()
    own_cache = pltpu.make_async_copy(cache_hbm.at[0], cache_buf.at[feat, row], own_sem)
    own_cache.start()

    barrier = pltpu.get_barrier_semaphore()
    pl.semaphore_signal(barrier, inc=1, device_id={"feat": partner}, device_id_type=MESH)
    for off in range(1, row_devs):
        pl.semaphore_signal(
            barrier, inc=1, device_id={"rows": lax.rem(row + off, row_devs)}, device_id_type=MESH
        )

    @pl.when(receives)
    def _():
        pl.semaphore_signal(barrier, inc=1, device_id={"section": section - 1}, device_id_type=MESH)

    @pl.when(sends)
    def _():
        pl.semaphore_signal(barrier, inc=1, device_id={"section": section + 1}, device_id_type=MESH)

    pl.semaphore_wait(
        barrier, row_devs + jnp.where(receives, 1, 0) + jnp.where(sends, 1, 0)
    )

    def x_copy(m, source):
        return pltpu.make_async_remote_copy(
            src_ref=rows_hbm.at[m, theirs], dst_ref=x_buf.at[m, source],
            send_sem=x_send.at[m], recv_sem=x_recv.at[m],
            device_id={"feat": partner}, device_id_type=MESH,
        )

    def cache_copy(off):
        return pltpu.make_async_remote_copy(
            src_ref=cache_hbm.at[0], dst_ref=cache_buf.at[feat, row],
            send_sem=cache_send.at[off - 1], recv_sem=cache_recv.at[row],
            device_id={"rows": lax.rem(row + off, row_devs)}, device_id_type=MESH,
        )

    def cache_arrival(off):
        source = lax.rem(row + off, row_devs)
        return pltpu.make_async_remote_copy(
            src_ref=cache_hbm.at[0], dst_ref=cache_buf.at[feat, source],
            send_sem=cache_send.at[off - 1], recv_sem=cache_recv.at[source],
            device_id={"rows": source}, device_id_type=MESH,
        )

    def cache_pass(off, source_feat):
        source = lax.rem(row + off, row_devs)
        return pltpu.make_async_remote_copy(
            src_ref=cache_hbm.at[0] if off == 0 else cache_buf.at[feat, source],
            dst_ref=cache_buf.at[source_feat, source],
            send_sem=pass_send.at[off], recv_sem=pass_recv.at[off],
            device_id={"feat": partner}, device_id_type=MESH,
        )

    @pl.when(first)
    def _():
        x_copy(0, feat).start()

    for off in range(1, row_devs):
        cache_copy(off).start()

    @pl.when(first)
    def _():
        for m in range(1, micro):
            x_copy(m, feat).start()

    cache_pass(0, feat).start()
    for copy in weights[1:]:
        copy.start()

    def h_copy(m, target):
        return pltpu.make_async_remote_copy(
            src_ref=h_out.at[m], dst_ref=h_buf.at[m],
            send_sem=h_send.at[m], recv_sem=h_recv.at[m],
            device_id={"section": target}, device_id_type=MESH,
        )

    def out_own(m):
        return pltpu.make_async_copy(staged.at[m, feat], hidden_hbm.at[0, m, mine], out_sem.at[m])

    def out_copy(m, place):
        return pltpu.make_async_remote_copy(
            src_ref=staged.at[m, partner], dst_ref=hidden_hbm.at[0, m, place],
            send_sem=out_send.at[m], recv_sem=out_recv.at[m],
            device_id={"feat": partner}, device_id_type=MESH,
        )

    groups = feats * gd
    pick_q = (iota((tokens, groups), 0) // rows_n == iota((tokens, groups), 1)).astype(F32)
    pick_k = (iota((groups, tokens), 1) // rows_n == iota((groups, tokens), 0)).astype(F32)
    pattern = (pattern_ref[...] != 0).astype(F32)
    seen = dot(dot(pick_q, pattern), pick_k) > 0.5
    qi, ki = iota((tokens, tokens), 0), iota((tokens, tokens), 1)
    seen = (seen | (qi == ki)) & (qi % rows_n == ki % rows_n)
    bias = jnp.where(seen, 0.0, EXCLUDED).astype(F32)
    feat_bias[:tokens] = bias
    feat_bias[tokens:] = bias
    item_bias[...] = jnp.where(
        iota((half, 2 * nk), 0) // rows_n == (iota((half, 2 * nk), 1) % nk) // train_n, 0.0, EXCLUDED
    ).astype(F32)

    def pass_cache():
        for off in range(1, row_devs):
            cache_arrival(off).wait_recv()
            cache_pass(off, feat).start()

    def stack_cache():
        own_cache.wait()
        for off in range(row_devs):
            cache_pass(off, partner).wait_recv()
        side = iota((nk, pair_w), 1) < pair_w // 2
        one = jnp.where(side, 1.0, 0.0).astype(BF16)
        other = jnp.where(side, 0.0, 1.0).astype(BF16)
        for f in range(feats):
            for kind in range(2):
                cache_wide[...] = cache_buf[f, :, kind].astype(F32).reshape(cache_wide.shape)
                for pair in range(pairs):
                    part = jnp.concatenate(
                        [cache_wide[pl.ds(pair * gd + g, train_n, stride=per_row), :] for g in range(gd)], axis=0
                    )
                    low = jnp.where(side, part, 0.0).astype(BF16)
                    high = jnp.where(side, 0.0, part).astype(BF16)
                    if kind == 0:
                        k_stack[f, pair, :nk] = low
                        k_stack[f, pair, nk:] = high
                    else:
                        v_stack[f, pair, :nk, :pair_w] = low
                        v_stack[f, pair, nk:, :pair_w] = high
                        v_stack[f, pair, :nk, pair_w:] = one
                        v_stack[f, pair, nk:, pair_w:] = other

    low_half = iota((tokens, pair_w), 1) < pair_w // 2
    low_lanes = iota((tokens, width), 1) % pair_w < pair_w // 2
    ones = jnp.ones((tokens, pair_w), BF16)

    tiles = [slice(pair * pair_w, (pair + 1) * pair_w) for pair in range(pairs)]

    def feature_mix(a, q, k):
        low = jnp.where(low_lanes, q, 0.0).astype(BF16)
        high = jnp.where(low_lanes, 0.0, q).astype(BF16)
        queries = [jnp.concatenate([low[:, lanes], high[:, lanes]], axis=0) for lanes in tiles]
        scores = [dot_t(q2, k[:, lanes]) for q2, lanes in zip(queries, tiles)]
        v = dot(a, wqkv[:, 2 * width :]).astype(BF16)
        scores = [s + feat_bias[...] for s in scores]
        tops = [jnp.max(s, axis=-1, keepdims=True) for s in scores]
        weights_of = [jnp.exp2(s - top).astype(BF16) for s, top in zip(scores, tops)]
        sums = [
            dot(p, jnp.concatenate([v[:, lanes], ones], axis=1)) for p, lanes in zip(weights_of, tiles)
        ]
        mixed = []
        for o in sums:
            total = jnp.where(low_half, o[:tokens, pair_w:], o[tokens:, pair_w:])
            o = jnp.where(low_half, o[:tokens, :pair_w], o[tokens:, :pair_w])
            mixed.append((o * pl.reciprocal(total, approx=True)).astype(BF16))
        return jnp.concatenate(mixed, axis=1)

    low_keys = iota((half, 2 * nk), 1) < nk

    def item_mix(query):
        units = [(f, pair) for f in range(feats) for pair in range(pairs)]
        scores = [
            dot_t(query[f * half : (f + 1) * half, tiles[pair]], k_stack[f, pair]) for f, pair in units
        ]
        scores = [s + item_bias[...] for s in scores]
        lows = [jnp.max(jnp.where(low_keys, s, -jnp.inf), axis=-1, keepdims=True) for s in scores]
        highs = [jnp.max(jnp.where(low_keys, -jnp.inf, s), axis=-1, keepdims=True) for s in scores]
        weights_of = [
            jnp.exp2(s - jnp.where(low_keys, low, high)).astype(BF16)
            for s, low, high in zip(scores, lows, highs)
        ]
        sums = [dot(p, v_stack[f, pair]) for p, (f, pair) in zip(weights_of, units)]
        mixed = [(o[:, :pair_w] * pl.reciprocal(o[:, pair_w:], approx=True)).astype(BF16) for o in sums]
        blocks = [jnp.concatenate(mixed[f * pairs : (f + 1) * pairs], axis=1) for f in range(feats)]
        return jnp.concatenate(blocks, axis=0)

    @pl.when(receives)
    def _():
        pass_cache()
        stack_cache()

    weights[0].wait()

    def spread(pair):
        return [
            pl.ds(f * block_n + pair * gd + g, rows_n, stride=per_row)
            for f in range(feats)
            for g in range(gd)
        ]

    def step(m, carry):
        @pl.when(first)
        def _():
            x_own(m).wait()
            x_copy(m, partner).wait_recv()
            wide[...] = x_buf[m].astype(F32).reshape(wide.shape)
            for pair in range(pairs):
                part = [wide[place, :] for place in spread(pair)]
                lanes = slice(pair * pair_w, (pair + 1) * pair_w)
                h_buf[m, :, lanes] = jnp.concatenate(part, axis=0).astype(BF16)

        @pl.when(receives)
        def _():
            h_copy(m, section - 1).wait_recv()

        @pl.when(m == 0)
        def _():
            for copy in weights[1:]:
                copy.wait()

        h = h_buf[m].astype(F32)
        a = normed(h, gains_ref[0, 0:1, :])
        q = dot(a, wqkv[:, :width]) * factor
        k = dot(a, wqkv[:, width : 2 * width]).astype(BF16)
        h1 = h + dot(feature_mix(a, q, k), wout[...])
        b = normed(h1, gains_ref[0, 1:2, :])
        query = (dot(b, wquery[...]) * factor).astype(BF16)

        @pl.when(first & (m == 0))
        def _():
            pass_cache()
            stack_cache()

        result = h1 + dot(item_mix(query), witem[...])
        h_out[m] = result.astype(BF16)

        @pl.when(sends)
        def _():
            h_copy(m, section + 1).start()

        for pair in range(pairs):
            for at, place in enumerate(spread(pair)):
                wide[place, :] = result[at * rows_n : (at + 1) * rows_n, pair * pair_w : (pair + 1) * pair_w]
        staged[m] = wide[...].reshape(feats, block_n, pair_w).astype(BF16)
        out_copy(m, mine).start()
        out_own(m).start()
        return carry

    lax.fori_loop(0, micro, step, 0)

    for m in range(micro):
        out_own(m).wait()
        out_copy(m, theirs).wait()

    @pl.when(first)
    def _():
        for m in range(micro):
            x_copy(m, feat).wait_send()

    @pl.when(sends)
    def _():
        for m in range(micro):
            h_copy(m, section + 1).wait_send()

    for off in range(1, row_devs):
        cache_copy(off).wait_send()
    for off in range(row_devs):
        cache_pass(off, feat).wait_send()


def per_device(sizes, test_rows, train_cache, pattern, feat_qkv, feat_out, item_query, item_out, gains):
    sections, row_devs = sizes
    micro, test_n, gd, width = test_rows.shape
    train_dev = train_cache.shape[2]
    feats = 2
    rows_n = test_n // feats
    tokens = test_n * gd
    nk = row_devs * train_dev * gd
    pair_w = 2 * (width // HEADS)
    pairs = width // pair_w
    anywhere = pl.BlockSpec(memory_space=pl.ANY)
    vmem = pl.BlockSpec(memory_space=pltpu.VMEM)
    dma = pltpu.SemaphoreType.DMA
    per_row = gd * pairs

    def as_rows(x):
        pieces = x.reshape(x.shape[:-1] + (pairs, pair_w)).swapaxes(-3, -2)
        return pieces.reshape(x.shape[:-3] + (x.shape[-3] * per_row, pair_w))

    hidden = pl.pallas_call(
        functools.partial(kernel, sizes),
        out_shape=jax.ShapeDtypeStruct((1, micro, test_n * per_row, pair_w), BF16),
        in_specs=[anywhere, anywhere, vmem, anywhere, anywhere, anywhere, anywhere, vmem],
        out_specs=anywhere,
        scratch_shapes=[
            pltpu.VMEM((micro, feats, rows_n * per_row, pair_w), BF16),
            pltpu.VMEM((width, 3 * width), BF16),
            pltpu.VMEM((width, width), BF16),
            pltpu.VMEM((width, width), BF16),
            pltpu.VMEM((width, width), BF16),
            pltpu.VMEM((micro, tokens, width), BF16),
            pltpu.VMEM((micro, tokens, width), BF16),
            pltpu.VMEM((feats, row_devs, 2, train_dev * per_row, pair_w), BF16),
            pltpu.VMEM((feats, pairs, 2 * nk, pair_w), BF16),
            pltpu.VMEM((feats, pairs, 2 * nk, 2 * pair_w), BF16),
            pltpu.VMEM((2 * tokens, tokens), F32),
            pltpu.VMEM((tokens // feats, 2 * nk), F32),
            pltpu.VMEM((micro, feats, rows_n * per_row, pair_w), BF16),
            pltpu.VMEM((test_n * per_row, pair_w), F32),
            pltpu.VMEM((row_devs * train_dev * per_row, pair_w), F32),
            dma((4,)),
            dma((micro,)),
            dma(()),
            dma((micro,)),
            dma((micro,)),
            dma((micro,)),
            dma((row_devs - 1,)),
            dma((row_devs,)),
            dma((row_devs,)),
            dma((row_devs,)),
            dma((micro,)),
            dma((micro,)),
            dma((micro,)),
            dma((micro,)),
        ],
        compiler_params=pltpu.CompilerParams(
            collective_id=0, has_side_effects=True, vmem_limit_bytes=VMEM_GRANT
        ),
    )(as_rows(test_rows), as_rows(train_cache), pattern, feat_qkv, feat_out, item_query, item_out, gains)
    hidden = hidden.reshape(1, micro, test_n, pairs, gd, pair_w).swapaxes(-3, -2)
    return hidden.reshape(1, micro, test_n, gd, width)


def solution(mesh):
    sizes = (mesh.shape["section"], mesh.shape["rows"])
    return jax.shard_map(
        functools.partial(per_device, sizes),
        mesh=mesh,
        in_specs=(
            P(None, ("groups", "rows"), "feat", None),
            P("section", None, ("groups", "rows"), "feat", None),
            P(),
            P("section", None, None),
            P("section", None, None),
            P("section", None, None),
            P("section", None, None),
            P("section", None, None),
        ),
        out_specs=P("section", None, ("groups", "rows"), "feat", None),
        check_vma=False,
    )
```
